256 devices in a mesh: seq: 32 (over x, y, core), help: 8 (over z).
Axes of the slice: x: 4, y: 4, z: 8, core: 2. Of those that a mesh axis runs over, the one named last changes fastest.
Arguments:
- queries: bfloat16 [16384, 4096], P('seq'), may hold values from -7 to 7
- keys_values: bfloat16 [16384, 2048], P('seq'), may hold values from -10 to 10
- verticals: int32 [32, 24], P('seq'), may hold values from 0 to 255, as said below
- slashes: int32 [32, 24], P('seq'), may hold values from 0 to 255, as said below
- units: int32 [32, 8, 192], P('seq', 'help'), may hold values from -1 to 1535, as said below
Outputs:
- attended: bfloat16 [16384, 4096], P(('seq', 'help'))
The draws below stay inside these ranges and needn't reach their ends.
Inputs may be any that keep to these rules, and one draw needn't show every extreme that they name: `verticals`: each head's 24 key tiles are distinct and ascending and include tile 0 and tile 256 - 1. `slashes`: each head's 24 offsets are distinct and ascending and include 0 and 255. Each list holds codes i * 6 + c in ascending order followed by -1 entries; a head's codes, each once, are units with an attended slot, among them the unit of the slot of slash offset 0 for every tile i; for some helper r, the head's lists of helpers r, r + 1, ... taken cyclically and joined in that order hold all its codes in ascending order, every list before the last nonempty one in that order holds 192 codes, and the lists after it are empty.
All inputs are finite; a program needn't handle non-finite values.
Results may differ from the reference program's by a relative error of at most 0.0042.
Values may be sent and summed in bfloat16 or wider, within the bound.
A program may use at most 128 MiB of HBM per device.

```python
import math
import jax
import jax.numpy as jnp
from jax import lax

HEADS = 32
KV_HEADS = 8
HEAD_DIM = 128
TILE = 64
TOKENS = 16384
NVERT = 24
GROUP = 8
NGROUP = 6
SLOTS = 192
N_HELP = 8


def slot_tiles_drawn(tile_rows, group_ids, vert_row, slash_row, group_size):
    nvert = vert_row.shape[0]
    slot_pos = group_ids[:, None] * group_size + jnp.arange(group_size, dtype=jnp.int32)[None, :]
    slot_table = jnp.concatenate([vert_row, slash_row])
    match_mask = slot_pos[..., None] == jnp.arange(2 * nvert, dtype=jnp.int32)[None, None, :]
    picked = jnp.sum(jnp.where(match_mask, slot_table[None, None, :], 0), axis=-1).astype(jnp.int32)
    is_vert = slot_pos < nvert
    row_tiles = tile_rows[:, None]
    covered = jnp.any((row_tiles - picked)[..., None] == slash_row[None, None, :], axis=-1)
    attended = jnp.where(is_vert, (picked <= row_tiles) & jnp.logical_not(covered), picked <= row_tiles)
    return attended


def tile_pattern(key):
    base_key = jax.random.fold_in(key, 101)
    n_tiles = TOKENS // TILE

    def pick_row(row_key):
        interior = jax.random.permutation(row_key, jnp.arange(1, n_tiles - 1, dtype=jnp.int32))[:NVERT - 2]
        return jnp.concatenate([jnp.zeros((1,), jnp.int32), jnp.sort(interior), jnp.full((1,), n_tiles - 1, jnp.int32)])
    vert_keys = jax.random.split(jax.random.fold_in(base_key, 1), HEADS)
    slash_keys = jax.random.split(jax.random.fold_in(base_key, 2), HEADS)
    return (jax.vmap(pick_row)(vert_keys), jax.vmap(pick_row)(slash_keys))


def draw_verticals(key, part):
    vert_rows, slash_rows = tile_pattern(key)
    return vert_rows


def draw_slashes(key, part):
    vert_rows, slash_rows = tile_pattern(key)
    return slash_rows


def draw_units(key, part):
    vert_rows, slash_rows = tile_pattern(key)
    key = jax.random.fold_in(key, 3)
    n_tiles = TOKENS // TILE
    rotate_key, keep_key = jax.random.split(key)
    rotate = jax.random.randint(rotate_key, (HEADS,), 0, N_HELP, dtype=jnp.int32)
    keep_draw = jax.random.randint(keep_key, (HEADS, n_tiles * NGROUP), 0, 10, dtype=jnp.int32) < 7
    tile_rows = jnp.repeat(jnp.arange(n_tiles, dtype=jnp.int32), NGROUP)
    group_ids = jnp.tile(jnp.arange(NGROUP, dtype=jnp.int32), n_tiles)

    def one_head(vert_row, slash_row, shift_by, keep_row):
        attended = slot_tiles_drawn(tile_rows, group_ids, vert_row, slash_row, GROUP)
        chosen = keep_row | (group_ids == NVERT // GROUP) | (tile_rows == n_tiles - 1)
        has_slot = jnp.any(attended, axis=1) & chosen
        rank_pos = jnp.cumsum(has_slot.astype(jnp.int32)) - 1
        helper = (shift_by + rank_pos // SLOTS) % N_HELP
        helper = jnp.where(has_slot, helper, N_HELP)
        slot_pos = jnp.maximum(rank_pos, 0) % SLOTS
        code_vals = tile_rows * NGROUP + group_ids
        list_table = jnp.full((N_HELP, SLOTS), -1, jnp.int32)
        return list_table.at[helper, slot_pos].set(code_vals, mode='drop')
    return jax.vmap(one_head)(vert_rows, slash_rows, rotate, keep_draw)


def draw_queries(key, part):
    key = jax.random.fold_in(key, 4)
    full_shape = (TOKENS, HEADS * HEAD_DIM)
    base_vals = jnp.clip(jax.random.normal(key, full_shape, jnp.float32), -6.0, 6.0)
    return base_vals.astype(jnp.bfloat16)


def draw_keys_values(key, part):
    key = jax.random.fold_in(key, 5)
    key_draw, value_draw, scale_draw = jax.random.split(key, 3)
    kv_width = KV_HEADS * HEAD_DIM
    row_scale = jnp.exp(jax.random.uniform(scale_draw, (TOKENS, 1), jnp.float32, math.log(0.32), math.log(3.2)))
    key_vals = jnp.clip(jax.random.normal(key_draw, (TOKENS, kv_width), jnp.float32), -6.0, 6.0)
    value_vals = jnp.clip(jax.random.normal(value_draw, (TOKENS, kv_width), jnp.float32), -3.0, 3.0) * row_scale
    return jnp.concatenate([key_vals, value_vals], axis=1).astype(jnp.bfloat16)


def setup_inputs(seed: int = 0) -> dict:
    key_list = jax.random.split(jax.random.key(seed), 6)
    return {
        "queries": draw_queries(jax.random.fold_in(key_list[5], 71), 0),
        "keys_values": draw_keys_values(jax.random.fold_in(key_list[5], 71), 0),
        "verticals": draw_verticals(jax.random.fold_in(key_list[5], 71), 0),
        "slashes": draw_slashes(jax.random.fold_in(key_list[5], 71), 0),
        "units": draw_units(jax.random.fold_in(key_list[5], 71), 0),
    }


NEG_FILL = -1.0e30


def slot_tiles(tile_rows, group_ids, vert_row, slash_row, group_size):
    nvert = vert_row.shape[0]
    slot_pos = group_ids[:, None] * group_size + jnp.arange(group_size, dtype=jnp.int32)[None, :]
    slot_table = jnp.concatenate([vert_row, slash_row])
    match_mask = slot_pos[..., None] == jnp.arange(2 * nvert, dtype=jnp.int32)[None, None, :]
    picked = jnp.sum(jnp.where(match_mask, slot_table[None, None, :], 0), axis=-1).astype(jnp.int32)
    is_vert = slot_pos < nvert
    row_tiles = tile_rows[:, None]
    covered = jnp.any((row_tiles - picked)[..., None] == slash_row[None, None, :], axis=-1)
    key_tile = jnp.where(is_vert, picked, row_tiles - picked).astype(jnp.int32)
    attended = jnp.where(is_vert, (picked <= row_tiles) & jnp.logical_not(covered), picked <= row_tiles)
    return key_tile, attended


def unit_partials(query_tiles, kv_tiles, tile_rows, group_ids, vert_row, slash_row):
    key_tile, attended = slot_tiles(tile_rows, group_ids, vert_row, slash_row, GROUP)
    safe_tile = jnp.clip(key_tile, 0, kv_tiles.shape[0] - 1).astype(jnp.int32)
    kv_picked = jnp.take(kv_tiles, safe_tile, axis=0).astype(jnp.float32)
    q_picked = jnp.take(query_tiles, tile_rows, axis=0).astype(jnp.float32)
    scores = jnp.einsum("uqd,ugkd->uqgk", q_picked, kv_picked[..., :HEAD_DIM]) * (HEAD_DIM ** -0.5)
    tile_len = query_tiles.shape[1]
    lower_mask = jnp.arange(tile_len)[None, :] <= jnp.arange(tile_len)[:, None]
    near_tile = (key_tile < tile_rows[:, None])[:, None, :, None]
    allowed = attended[:, None, :, None] & (near_tile | lower_mask[None, :, None, :])
    masked = jnp.where(allowed, scores, NEG_FILL)
    row_max = jnp.max(masked, axis=(2, 3))
    exp_terms = jnp.exp(masked - row_max[:, :, None, None])
    row_sum = jnp.sum(exp_terms, axis=(2, 3))
    weights = lax.optimization_barrier(exp_terms.astype(jnp.bfloat16)).astype(jnp.float32)
    outputs = jnp.einsum("uqgk,ugkd->uqd", weights, kv_picked[..., HEAD_DIM:])
    return row_max, row_sum, outputs


def reference(queries, keys_values, verticals, slashes, units):
    tokens = queries.shape[0]
    n_tiles = tokens // TILE
    query_cube = queries.reshape(tokens, HEADS, HEAD_DIM)
    kv_split = keys_values.reshape(tokens, 2, KV_HEADS, HEAD_DIM)
    kv_joined = jnp.concatenate([kv_split[:, 0], kv_split[:, 1]], axis=-1)

    def one_head(head_pos):
        group_index = head_pos // (HEADS // KV_HEADS)
        query_tiles = jnp.take(query_cube, head_pos, axis=1).reshape(n_tiles, TILE, HEAD_DIM)
        kv_tiles = jnp.take(kv_joined, group_index, axis=1).reshape(n_tiles, TILE, 2 * HEAD_DIM)
        vert_row = jnp.take(verticals, head_pos, axis=0)
        slash_row = jnp.take(slashes, head_pos, axis=0)
        list_table = jnp.take(units, head_pos, axis=0)

        def one_list(code_list):
            active = code_list >= 0
            safe_code = jnp.maximum(code_list, 0).astype(jnp.int32)
            tile_rows = (safe_code // NGROUP).astype(jnp.int32)
            group_ids = (safe_code % NGROUP).astype(jnp.int32)
            row_max, row_sum, outputs = unit_partials(query_tiles, kv_tiles, tile_rows, group_ids, vert_row, slash_row)
            row_max = jnp.where(active[:, None], row_max, 3.0 * NEG_FILL)
            return tile_rows, row_max, row_sum, outputs

        tile_rows, row_max, row_sum, outputs = lax.map(one_list, list_table)
        tile_rows = tile_rows.reshape(-1)
        row_max = row_max.reshape(-1, TILE)
        row_sum = row_sum.reshape(-1, TILE)
        outputs = outputs.reshape(-1, TILE, HEAD_DIM)
        peak_max = jax.ops.segment_max(row_max, tile_rows, num_segments=n_tiles)
        scale_w = jnp.exp(row_max - jnp.take(peak_max, tile_rows, axis=0))
        numerator = jax.ops.segment_sum(outputs * scale_w[..., None], tile_rows, num_segments=n_tiles)
        denominator = jax.ops.segment_sum(row_sum * scale_w, tile_rows, num_segments=n_tiles)
        head_out = numerator / denominator[..., None]
        return head_out.astype(jnp.bfloat16).reshape(tokens, HEAD_DIM)

    per_head = lax.map(one_head, jnp.arange(HEADS, dtype=jnp.int32))
    return jnp.transpose(per_head, (1, 0, 2)).reshape(tokens, HEADS * HEAD_DIM)
```

```python
import functools

import jax
import jax.numpy as jnp
from jax import lax
from jax.experimental import pallas as pl
from jax.experimental.pallas import tpu as pltpu
from jax.sharding import PartitionSpec as P

HEADS = 32
KV_HEADS = 8
HEAD_DIM = 128
TILE = 64
NVERT = 24
NGROUP = 6
GROUP_HEADS = 4
TILES_LOCAL = 8
KEYS = NVERT * TILE
CHUNK = 256
CHUNK_TILES = CHUNK // TILE
NCHUNK = KEYS // CHUNK
ROWS = TILES_LOCAL * TILE
NEG = -1e30
EXP_SCALE = HEAD_DIM ** -0.5 * 1.4426950408889634


def dot_t(a, b):
    return lax.dot_general(a, b, (((1,), (1,)), ((), ())), preferred_element_type=jnp.float32)


def make_bias(first_tile, lists, vs_ref, bias_v, bias_s):
    lane = lax.broadcasted_iota(jnp.int32, (TILES_LOCAL, 128), 1)
    tile = lax.broadcasted_iota(jnp.int32, (TILES_LOCAL, 128), 0) + first_tile
    slot_of = lax.broadcasted_iota(jnp.int32, (128, KEYS), 1) // TILE
    spread = jnp.where(slot_of == lax.broadcasted_iota(jnp.int32, (128, KEYS), 0), 1.0, 0.0).astype(jnp.bfloat16)
    width = lists.shape[-1]
    row_tile = lax.broadcasted_iota(jnp.int32, (TILES_LOCAL, width), 0) + first_tile
    for k in range(GROUP_HEADS):
        total = jnp.zeros((TILES_LOCAL, width), jnp.int32)
        for r in range(lists.shape[1]):
            code = jnp.broadcast_to(lists[k, r:r + 1, :], (TILES_LOCAL, width))
            group = code - row_tile * NGROUP
            total += jnp.where((group >= 0) & (group < NGROUP), lax.shift_left(1, jnp.clip(group, 0, NGROUP - 1)), 0)
        named = jnp.sum(total, axis=1, keepdims=True)
        vert = jnp.broadcast_to(vs_ref[k:k + 1, :], (TILES_LOCAL, 128))
        slash = jnp.broadcast_to(vs_ref[GROUP_HEADS + k:GROUP_HEADS + k + 1, :], (TILES_LOCAL, 128))
        covered = jnp.zeros((TILES_LOCAL, 128), jnp.bool_)
        for n in range(NVERT):
            covered |= (tile - vert) == slash[:, n:n + 1]
        unit = lane // 8
        bit_v = lax.shift_right_logical(jnp.broadcast_to(named, unit.shape), jnp.minimum(unit, 2)) & 1
        bit_s = lax.shift_right_logical(jnp.broadcast_to(named, unit.shape), jnp.minimum(unit + 3, 5)) & 1
        real = lane < NVERT
        att_v = real & (vert <= tile) & jnp.logical_not(covered) & (bit_v == 1)
        att_s = real & (slash <= tile) & (bit_s == 1)
        for att, bias in ((att_v, bias_v), (att_s, bias_s)):
            hot = jnp.where(att, 1.0, 0.0).astype(jnp.bfloat16)
            wide = jnp.dot(hot, spread, preferred_element_type=jnp.float32)
            bias[k] = ((wide - 1.0) * (-NEG)).reshape(TILES_LOCAL, 1, KEYS)


def tiles_of(ref, places):
    return jnp.concatenate([ref[pl.ds(pl.multiple_of(p * TILE, TILE), TILE), :] for p in places], axis=0)


def score_head(k, first_tile, q_ref, k_ref, verts, slashes, bias_v, bias_s, score_v, p_v, p_s, ell):
    q_cols = pl.ds(pl.multiple_of(k * HEAD_DIM, HEAD_DIM), HEAD_DIM)
    for c in range(NCHUNK):
        keys = tiles_of(k_ref, [verts[k, c * CHUNK_TILES + n] for n in range(CHUNK_TILES)])
        s = dot_t(q_ref[:, q_cols], keys)
        cols = slice(c * CHUNK, (c + 1) * CHUNK)
        s = s.reshape(TILES_LOCAL, TILE, CHUNK) + bias_v[k, :, :, cols]
        score_v[:, cols] = s.reshape(ROWS, CHUNK)
    row = lax.broadcasted_iota(jnp.int32, (TILE, CHUNK), 0)
    col = lax.broadcasted_iota(jnp.int32, (TILE, CHUNK), 1)
    diagonal = jnp.where((col < TILE) & (col > row), NEG, 0.0)

    @pl.loop(0, TILES_LOCAL)
    def _(t):
        rows = pl.ds(pl.multiple_of(t * TILE, TILE), TILE)
        q = q_ref[rows, q_cols]
        parts = []
        for c in range(NCHUNK):
            places = [jnp.maximum(first_tile + t - slashes[k, c * CHUNK_TILES + n], 0) for n in range(CHUNK_TILES)]
            s = dot_t(q, tiles_of(k_ref, places))
            s = s + bias_s[k, t, :, c * CHUNK:(c + 1) * CHUNK]
            if c == 0:
                s = s + diagonal
            parts.append(s)
        for c in range(NCHUNK):
            parts.append(score_v[rows, c * CHUNK:(c + 1) * CHUNK])
        peak = functools.reduce(jnp.maximum, parts)
        peak = jnp.max(peak, axis=1, keepdims=True)
        total = jnp.zeros((TILE, CHUNK), jnp.float32)
        for c, s in enumerate(parts):
            p = jnp.exp2((s - peak) * EXP_SCALE)
            total += p
            out = p_s if c < NCHUNK else p_v
            cc = c % NCHUNK
            out[k, rows, cc * CHUNK:(cc + 1) * CHUNK] = p.astype(jnp.bfloat16)
        ell[k, rows, :] = jnp.broadcast_to(jnp.sum(total, axis=1, keepdims=True), (TILE, HEAD_DIM))


def value_head(k, first_tile, v_ref, verts, slashes, p_v, p_s, ell, acc, out_ref):
    values = tiles_of(v_ref, [verts[k, n] for n in range(NVERT)])
    acc[...] = jnp.dot(p_v[k], values, preferred_element_type=jnp.float32)
    out_cols = pl.ds(pl.multiple_of(k * HEAD_DIM, HEAD_DIM), HEAD_DIM)

    @pl.loop(0, TILES_LOCAL)
    def _(t):
        rows = pl.ds(pl.multiple_of(t * TILE, TILE), TILE)
        places = [jnp.maximum(first_tile + t - slashes[k, n], 0) for n in range(NVERT)]
        o = jnp.dot(p_s[k, rows, :], tiles_of(v_ref, places), preferred_element_type=jnp.float32)
        out_ref[rows, out_cols] = ((o + acc[rows, :]) / ell[k, rows, :]).astype(jnp.bfloat16)


def attend_kernel(first_ref, verts, slashes, vs_ref, lists, q_ref, k_ref, v_ref, out_ref,
                  bias_v, bias_s, score_v, p_v, p_s, ell, acc):
    first_tile = first_ref[0]
    make_bias(first_tile, lists, vs_ref, bias_v, bias_s)

    @pl.loop(0, GROUP_HEADS)
    def _(k):
        score_head(k, first_tile, q_ref, k_ref, verts, slashes, bias_v, bias_s, score_v, p_v, p_s, ell)

    @pl.loop(0, GROUP_HEADS)
    def _(k):
        value_head(k, first_tile, v_ref, verts, slashes, p_v, p_s, ell, acc, out_ref)


def scratch():
    return [
        pltpu.VMEM((GROUP_HEADS, TILES_LOCAL, 1, KEYS), jnp.float32),
        pltpu.VMEM((GROUP_HEADS, TILES_LOCAL, 1, KEYS), jnp.float32),
        pltpu.VMEM((ROWS, KEYS), jnp.float32),
        pltpu.VMEM((GROUP_HEADS, ROWS, KEYS), jnp.bfloat16),
        pltpu.VMEM((GROUP_HEADS, ROWS, KEYS), jnp.bfloat16),
        pltpu.VMEM((GROUP_HEADS, ROWS, HEAD_DIM), jnp.float32),
        pltpu.VMEM((ROWS, HEAD_DIM), jnp.float32),
    ]


def attend(first, verts, slashes, vs, lists, q, keys, values):
    smem = pl.BlockSpec(memory_space=pltpu.SMEM)
    vmem = pl.BlockSpec(memory_space=pltpu.VMEM)
    return pl.pallas_call(
        attend_kernel,
        out_shape=jax.ShapeDtypeStruct((ROWS, GROUP_HEADS * HEAD_DIM), jnp.bfloat16),
        in_specs=[smem, smem, smem, vmem, vmem, vmem, vmem, vmem],
        out_specs=vmem,
        scratch_shapes=scratch(),
        compiler_params=pltpu.CompilerParams(vmem_limit_bytes=56 * 1024 * 1024),
        name="attend",
    )(first, verts, slashes, vs, lists, q, keys, values)


def per_device(queries, keys_values, verticals, slashes, units):
    s = lax.axis_index("seq")
    z = lax.axis_index("help")
    kv_cols = KV_HEADS * HEAD_DIM
    local_k = lax.dynamic_slice_in_dim(keys_values, z * HEAD_DIM, HEAD_DIM, 1)
    local_v = lax.dynamic_slice_in_dim(keys_values, kv_cols + z * HEAD_DIM, HEAD_DIM, 1)
    q = lax.dynamic_slice_in_dim(queries, z * GROUP_HEADS * HEAD_DIM, GROUP_HEADS * HEAD_DIM, 1)
    lists = lax.all_gather(units[0, 0], "help", axis=0)
    plan = jnp.concatenate([lists.reshape(-1), verticals[0], slashes[0]])
    plan = lax.all_gather(plan, "seq", axis=0)
    plan = lax.dynamic_slice_in_dim(plan, z * GROUP_HEADS, GROUP_HEADS, 0)
    n_list = lists.size
    lists = plan[:, :n_list].reshape((GROUP_HEADS,) + lists.shape)
    verts = plan[:, n_list:n_list + NVERT]
    slash = plan[:, n_list + NVERT:]
    vs = jnp.pad(jnp.concatenate([verts, slash]), ((0, 0), (0, 128 - NVERT)))
    keys = lax.all_gather(local_k, "seq", axis=0, tiled=True)
    values = lax.all_gather(local_v, "seq", axis=0, tiled=True)
    first = jnp.full((1,), s * TILES_LOCAL, jnp.int32)
    out = attend(first, verts, slash, vs, lists, q, keys, values)
    return lax.all_to_all(out, "help", split_axis=0, concat_axis=1, tiled=True)


def solution(mesh):
    in_specs = (
        P("seq", None),
        P("seq", None),
        P("seq", None),
        P("seq", None),
        P("seq", "help", None),
    )
    out_specs = P(("seq", "help"), None)
    return jax.shard_map(
        per_device, mesh=mesh, in_specs=in_specs, out_specs=out_specs, check_vma=False
    )
```

```python
import functools

import jax
import jax.numpy as jnp
from jax import lax
from jax.experimental import pallas as pl
from jax.experimental.pallas import tpu as pltpu
from jax.sharding import PartitionSpec as P

HEADS = 32
KV_HEADS = 8
HEAD_DIM = 128
TILE = 64
NVERT = 24
NGROUP = 6
GROUP_HEADS = 4
TILES_LOCAL = 8
KEYS = NVERT * TILE
CHUNK = 256
CHUNK_TILES = CHUNK // TILE
NCHUNK = KEYS // CHUNK
ROWS = TILES_LOCAL * TILE
NEG = -1e30
HALF = ROWS // 2
MESH = pl.DeviceIdType.MESH
EXP_SCALE = HEAD_DIM ** -0.5 * 1.4426950408889634


def dot_t(a, b):
    return lax.dot_general(a, b, (((1,), (1,)), ((), ())), preferred_element_type=jnp.float32)


def make_bias(first_tile, plan, bias_v, bias_s):
    lane = lax.broadcasted_iota(jnp.int32, (TILES_LOCAL, 128), 1)
    tile = lax.broadcasted_iota(jnp.int32, (TILES_LOCAL, 128), 0) + first_tile
    slot_of = lax.broadcasted_iota(jnp.int32, (128, KEYS), 1) // TILE
    spread = jnp.where(slot_of == lax.broadcasted_iota(jnp.int32, (128, KEYS), 0), 1.0, 0.0).astype(jnp.bfloat16)
    for k in range(GROUP_HEADS):
        named = jnp.zeros((TILES_LOCAL, 128), jnp.int32)
        for n in range(2):
            mask = jnp.broadcast_to(plan[k, n:n + 1, :], (TILES_LOCAL, 128))
            named += jnp.where(lane + n * 128 == tile, mask, 0)
        named = jnp.sum(named, axis=1, keepdims=True)
        vert = jnp.broadcast_to(plan[k, 2:3, :], (TILES_LOCAL, 128))
        slash = jnp.broadcast_to(plan[k, 3:4, :], (TILES_LOCAL, 128))
        covered = jnp.zeros((TILES_LOCAL, 128), jnp.bool_)
        for n in range(NVERT):
            covered |= (tile - vert) == slash[:, n:n + 1]
        unit = lane // 8
        bit_v = lax.shift_right_logical(jnp.broadcast_to(named, unit.shape), jnp.minimum(unit, 2)) & 1
        bit_s = lax.shift_right_logical(jnp.broadcast_to(named, unit.shape), jnp.minimum(unit + 3, 5)) & 1
        real = lane < NVERT
        att_v = real & (vert <= tile) & jnp.logical_not(covered) & (bit_v == 1)
        att_s = real & (slash <= tile) & (bit_s == 1)
        for att, bias in ((att_v, bias_v), (att_s, bias_s)):
            hot = jnp.where(att, 1.0, 0.0).astype(jnp.bfloat16)
            wide = jnp.dot(hot, spread, preferred_element_type=jnp.float32)
            bias[k] = ((wide - 1.0) * (-NEG)).reshape(TILES_LOCAL, 1, KEYS)


def tile_of(ref, place):
    shard = lax.shift_right_logical(place, 3)
    row = (place & (TILES_LOCAL - 1)) * TILE
    return ref[shard, pl.ds(row, TILE), :]


def tiles_of(ref, places):
    return jnp.concatenate([tile_of(ref, p) for p in places], axis=0)


def score_head(k, first_tile, q_ref, k_ref, slots, bias_v, bias_s, score_v, p_v, p_s, ell):
    q_cols = pl.ds(pl.multiple_of(k * HEAD_DIM, HEAD_DIM), HEAD_DIM)
    for c in range(NCHUNK):
        keys = tiles_of(k_ref, [slots[k, 2, c * CHUNK_TILES + n] for n in range(CHUNK_TILES)])
        s = dot_t(q_ref[:, q_cols], keys)
        cols = slice(c * CHUNK, (c + 1) * CHUNK)
        s = s.reshape(TILES_LOCAL, TILE, CHUNK) + bias_v[k, :, :, cols]
        score_v[:, cols] = s.reshape(ROWS, CHUNK)
    row = lax.broadcasted_iota(jnp.int32, (TILE, CHUNK), 0)
    col = lax.broadcasted_iota(jnp.int32, (TILE, CHUNK), 1)
    diagonal = jnp.where((col < TILE) & (col > row), NEG, 0.0)

    @pl.loop(0, TILES_LOCAL)
    def _(t):
        rows = pl.ds(pl.multiple_of(t * TILE, TILE), TILE)
        q = q_ref[rows, q_cols]
        parts = []
        for c in range(NCHUNK):
            places = [jnp.maximum(first_tile + t - slots[k, 3, c * CHUNK_TILES + n], 0) for n in range(CHUNK_TILES)]
            s = dot_t(q, tiles_of(k_ref, places))
            s = s + bias_s[k, t, :, c * CHUNK:(c + 1) * CHUNK]
            if c == 0:
                s = s + diagonal
            parts.append(s)
        for c in range(NCHUNK):
            parts.append(score_v[rows, c * CHUNK:(c + 1) * CHUNK])
        peak = functools.reduce(jnp.maximum, parts)
        peak = jnp.max(peak, axis=1, keepdims=True)
        total = jnp.zeros((TILE, CHUNK), jnp.float32)
        for c, s in enumerate(parts):
            p = jnp.exp2((s - peak) * EXP_SCALE)
            total += p
            out = p_s if c < NCHUNK else p_v
            cc = c % NCHUNK
            out[k, rows, cc * CHUNK:(cc + 1) * CHUNK] = p.astype(jnp.bfloat16)
        ell[k, rows, :] = jnp.broadcast_to(jnp.sum(total, axis=1, keepdims=True), (TILE, HEAD_DIM))


def value_head(k, first_tile, v_ref, slots, p_v, p_s, ell, acc, out_buf):
    values = tiles_of(v_ref, [slots[k, 2, n] for n in range(NVERT)])
    acc[...] = jnp.dot(p_v[k], values, preferred_element_type=jnp.float32)

    @pl.loop(0, TILES_LOCAL)
    def _(t):
        rows = pl.ds(pl.multiple_of(t * TILE, TILE), TILE)
        places = [jnp.maximum(first_tile + t - slots[k, 3, n], 0) for n in range(NVERT)]
        o = jnp.dot(p_s[k, rows, :], tiles_of(v_ref, places), preferred_element_type=jnp.float32)
        out_buf[k, rows, :] = ((o + acc[rows, :]) / ell[k, rows, :]).astype(jnp.bfloat16)


class Gather:
    def __init__(self, me, z, buf, rows, send, recv):
        self.me, self.z, self.buf, self.rows, self.send, self.recv = me, z, buf, rows, send, recv
        self.core = me % 2
        x, y = me // 8, (me // 2) % 4
        c = self.core
        self.a = x * (1 - c) + y * c
        self.b = y * (1 - c) + x * c
        self.started = []

    def at(self, da, db):
        c = self.core
        a, b = (self.a + da) % 4, (self.b + db) % 4
        x = a * (1 - c) + b * c
        y = b * (1 - c) + a * c
        return (x * 4 + y) * 2 + c

    def sibling(self, shard):
        return shard + 1 - 2 * self.core

    def region(self, shard, half):
        if half is None:
            return self.buf.at[shard]
        if half == 0:
            return self.buf.at[shard, pl.ds(0, HALF)]
        return self.buf.at[shard, pl.ds(HALF, self.rows - HALF)]

    def copy(self, shard, half, target, n):
        region = self.region(shard, half)
        return pltpu.make_async_remote_copy(
            src_ref=region, dst_ref=region, send_sem=self.send.at[n],
            recv_sem=self.recv.at[shard, 0 if half is None else half],
            device_id=(target, self.z), device_id_type=MESH)

    def put(self, shard, half, target):
        copy = self.copy(shard, half, target, len(self.started))
        copy.start()
        self.started.append(copy)

    def got(self, shard, half):
        self.copy(shard, half, self.sibling(self.me), 0).wait_recv()

    def put_a(self, shard, half, da):
        self.put(shard, half, self.at(da, 0))

    def put_b(self, shard, half, way=None):
        for db in (1, -1) if way is None else (way,):
            self.put(shard, half, self.at(0, db))

    def across(self, shard):
        self.put(shard, None, self.sibling(self.me))

    def own(self, half):
        mine = self.me
        self.put_a(mine, half, 1)
        self.put_a(mine, half, -1)
        self.put_b(mine, half)

    def first(self):
        left, right = self.at(-1, 0), self.at(1, 0)
        self.got(left, 0)
        self.put_a(left, 0, 1)
        self.got(right, 0)
        self.got(right, 1)
        self.put_a(right, 1, -1)
        self.got(left, 1)
        for shard in (left, right):
            for half in (0, 1):
                self.put_b(shard, half)
            self.across(shard)

    def second(self):
        far = self.at(2, 0)
        for half in (0, 1):
            self.got(far, half)
            self.put_b(far, half)
        self.across(far)

    def third(self, da):
        down, up = self.at(da, -1), self.at(da, 1)
        self.got(down, 0)
        self.put_b(down, 0, 1)
        self.got(up, 0)
        self.got(up, 1)
        self.put_b(up, 1, -1)
        self.got(down, 1)
        self.across(down)
        self.across(up)

    def fourth(self, da):
        far = self.at(da, 2)
        self.got(far, 0)
        self.got(far, 1)
        self.across(far)

    def stages(self):
        return [
            self.first, lambda: self.third(0), self.second, lambda: self.third(-1), lambda: self.fourth(0),
            lambda: self.third(1), lambda: self.fourth(-1), lambda: self.third(2), lambda: self.fourth(1),
            lambda: self.fourth(2),
        ]

    def last(self):
        for da in range(4):
            for db in range(4):
                self.got(self.sibling(self.at(da, db)), None)

    def drain(self):
        for copy in self.started:
            copy.wait_send()


N_SENDS = 46
N_SEQ = 32


def fused_kernel(q_hbm, kv_hbm, vs_ref, codes_ref, out_ref,
                 k_buf, v_buf, q_ref, parts, plan, slots, bias_v, bias_s, score_v, p_v, p_s, ell, acc, out_buf,
                 local_sem, part_send, part_recv, plan_send, plan_recv, k_send, k_recv, v_send, v_recv, out_send, out_recv):
    me = lax.axis_index("seq")
    z = lax.axis_index("help")
    keys = Gather(me, z, k_buf, ROWS, k_send, k_recv)
    values = Gather(me, z, v_buf, ROWS, v_send, v_recv)
    first_tile = me * TILES_LOCAL
    owner = me // GROUP_HEADS

    barrier = pltpu.get_barrier_semaphore()
    peers = [(keys.at(1, 0), z), (keys.at(-1, 0), z), (keys.at(0, 1), z), (keys.at(0, -1), z), (keys.sibling(me), z)]
    peers += [(me, (z + n) % 8) for n in range(1, 8)]
    for peer in peers:
        pl.semaphore_signal(barrier, inc=1, device_id=peer, device_id_type=MESH)
    for k in range(GROUP_HEADS):
        @pl.when(me != z * GROUP_HEADS + k)
        def _():
            pl.semaphore_signal(barrier, inc=1, device_id=(z * GROUP_HEADS + k, z), device_id_type=MESH)

    k_cols = pl.ds(pl.multiple_of(z * HEAD_DIM, HEAD_DIM), HEAD_DIM)
    v_cols = pl.ds(pl.multiple_of(z * HEAD_DIM + KV_HEADS * HEAD_DIM, HEAD_DIM), HEAD_DIM)
    q_cols = pl.ds(pl.multiple_of(z * GROUP_HEADS * HEAD_DIM, GROUP_HEADS * HEAD_DIM), GROUP_HEADS * HEAD_DIM)
    k_local = pltpu.make_async_copy(kv_hbm.at[:, k_cols], k_buf.at[me, pl.ds(0, ROWS)], local_sem.at[0])
    v_local = pltpu.make_async_copy(kv_hbm.at[:, v_cols], v_buf.at[me], local_sem.at[1])
    q_local = pltpu.make_async_copy(q_hbm.at[:, q_cols], q_ref, local_sem.at[2])
    k_local.start()
    v_local.start()
    q_local.start()

    width = codes_ref.shape[1]
    tile = lax.broadcasted_iota(jnp.int32, (128, width), 0)
    eye = lax.broadcasted_iota(jnp.int32, (128, 128), 0) == lax.broadcasted_iota(jnp.int32, (128, 128), 1)
    named = []
    for n in range(2):
        group = jnp.broadcast_to(codes_ref[...], (128, width)) - (tile + n * 128) * NGROUP
        bits = jnp.where((group >= 0) & (group < NGROUP), lax.shift_left(1, jnp.clip(group, 0, NGROUP - 1)), 0)
        column = jnp.sum(bits, axis=1, keepdims=True)
        named.append(jnp.sum(jnp.where(eye, jnp.broadcast_to(column, (128, 128)), 0), axis=0, keepdims=True))
    parts[z] = jnp.concatenate(named + [jnp.zeros((6, 128), jnp.int32)], axis=0)

    @pl.when(z != owner)
    def _():
        pl.semaphore_wait(barrier, len(peers))

    @pl.when(z == owner)
    def _():
        pl.semaphore_wait(barrier, len(peers) + N_SEQ - 1)

    part = pltpu.make_async_remote_copy(
        src_ref=parts.at[z], dst_ref=parts.at[z], send_sem=part_send, recv_sem=part_recv.at[z],
        device_id=(me, owner), device_id_type=MESH)

    @pl.when(z != owner)
    def _():
        part.start()

    k_local.wait()
    keys.own(0)
    keys.own(1)
    keys.across(me)
    v_local.wait()
    mine = me % GROUP_HEADS

    def plan_copy(k, n):
        return pltpu.make_async_remote_copy(
            src_ref=plan.at[k], dst_ref=plan.at[k], send_sem=plan_send.at[n], recv_sem=plan_recv.at[k],
            device_id=((me + n) % N_SEQ, z), device_id_type=MESH)

    @pl.when(z != owner)
    def _():
        part.wait_send()

    @pl.when(z == owner)
    def _():
        for n in range(1, 8):
            other = (z + n) % 8
            pltpu.make_async_remote_copy(
                src_ref=parts.at[other], dst_ref=parts.at[other], send_sem=part_send, recv_sem=part_recv.at[other],
                device_id=(me, other), device_id_type=MESH).wait_recv()
        total = parts[0]
        for n in range(1, 8):
            total += parts[n]
        plan[mine] = jnp.concatenate([total[:2], vs_ref[...], jnp.zeros((4, 128), jnp.int32)], axis=0)
        for n in range(1, N_SEQ):
            plan_copy(mine, n).start()

    for stage in keys.stages():
        stage()
    values.own(0)
    values.own(1)
    values.across(me)
    keys.last()

    for k in range(GROUP_HEADS):
        @pl.when(me != z * GROUP_HEADS + k)
        def _():
            plan_copy(k, 1).wait_recv()
    slots_copy = pltpu.make_async_copy(plan, slots, local_sem.at[3])
    slots_copy.start()
    make_bias(first_tile, plan, bias_v, bias_s)
    slots_copy.wait()
    q_local.wait()

    stages = values.stages()
    for k in range(GROUP_HEADS):
        score_head(k, first_tile, q_ref, k_buf, slots, bias_v, bias_s, score_v, p_v, p_s, ell)
        for stage in stages[:3]:
            stage()
        stages = stages[3:]
    values.last()

    sent = []
    for k in range(GROUP_HEADS):
        value_head(k, first_tile, v_buf, slots, p_v, p_s, ell, acc, out_buf)
        cols = pl.ds(pl.multiple_of((z * GROUP_HEADS + k) * HEAD_DIM, HEAD_DIM), HEAD_DIM)
        for n in range(1, 8):
            other = (z + n) % 8
            copy = pltpu.make_async_remote_copy(
                src_ref=out_buf.at[k, pl.ds(pl.multiple_of(other * TILE, TILE), TILE)], dst_ref=out_ref.at[:, cols],
                send_sem=out_send.at[k, n], recv_sem=out_recv.at[z, k], device_id=(me, other), device_id_type=MESH)
            copy.start()
            sent.append(copy)
        out_ref[:, cols] = out_buf[k, pl.ds(pl.multiple_of(z * TILE, TILE), TILE), :]
    for k in range(GROUP_HEADS):
        for n in range(1, 8):
            other = (z + n) % 8
            cols = pl.ds(pl.multiple_of((other * GROUP_HEADS + k) * HEAD_DIM, HEAD_DIM), HEAD_DIM)
            pltpu.make_async_remote_copy(
                src_ref=out_buf.at[k, pl.ds(0, TILE)], dst_ref=out_ref.at[:, cols],
                send_sem=out_send.at[k, n], recv_sem=out_recv.at[other, k], device_id=(me, other),
                device_id_type=MESH).wait_recv()
    for copy in sent:
        copy.wait_send()
    keys.drain()
    values.drain()

    @pl.when(z == owner)
    def _():
        for n in range(1, N_SEQ):
            plan_copy(mine, n).wait_send()


def per_device(queries, keys_values, verticals, slashes, units):
    vs = jnp.pad(jnp.concatenate([verticals, slashes]), ((0, 0), (0, 128 - NVERT)))
    vmem = pl.BlockSpec(memory_space=pltpu.VMEM)
    hbm = pl.BlockSpec(memory_space=pl.ANY)
    dma = pltpu.SemaphoreType.DMA
    seq = lax.axis_size("seq")
    return pl.pallas_call(
        fused_kernel,
        out_shape=jax.ShapeDtypeStruct((TILE, HEADS * HEAD_DIM), jnp.bfloat16),
        in_specs=[hbm, hbm, vmem, vmem],
        out_specs=vmem,
        scratch_shapes=[
            pltpu.VMEM((seq, ROWS, HEAD_DIM), jnp.bfloat16),
            pltpu.VMEM((seq, ROWS, HEAD_DIM), jnp.bfloat16),
            pltpu.VMEM((ROWS, GROUP_HEADS * HEAD_DIM), jnp.bfloat16),
            pltpu.VMEM((8, 8, 128), jnp.int32),
            pltpu.VMEM((GROUP_HEADS, 8, 128), jnp.int32),
            pltpu.SMEM((GROUP_HEADS, 8, 128), jnp.int32),
            pltpu.VMEM((GROUP_HEADS, TILES_LOCAL, 1, KEYS), jnp.float32),
            pltpu.VMEM((GROUP_HEADS, TILES_LOCAL, 1, KEYS), jnp.float32),
            pltpu.VMEM((ROWS, KEYS), jnp.float32),
            pltpu.VMEM((GROUP_HEADS, ROWS, KEYS), jnp.bfloat16),
            pltpu.VMEM((GROUP_HEADS, ROWS, KEYS), jnp.bfloat16),
            pltpu.VMEM((GROUP_HEADS, ROWS, HEAD_DIM), jnp.float32),
            pltpu.VMEM((ROWS, HEAD_DIM), jnp.float32),
            pltpu.VMEM((GROUP_HEADS, ROWS, HEAD_DIM), jnp.bfloat16),
            dma((4,)), dma, dma((8,)), dma((N_SEQ,)), dma((GROUP_HEADS,)),
            dma((N_SENDS,)), dma((seq, 2)), dma((N_SENDS,)), dma((seq, 2)),
            dma((GROUP_HEADS, 8)), dma((8, GROUP_HEADS)),
        ],
        compiler_params=pltpu.CompilerParams(
            vmem_limit_bytes=56 * 1024 * 1024, collective_id=0, has_side_effects=True),
        name="fused_attention",
    )(queries, keys_values, vs, units[0])


def solution(mesh):
    in_specs = (
        P("seq", None),
        P("seq", None),
        P("seq", None),
        P("seq", None),
        P("seq", "help", None),
    )
    out_specs = P(("seq", "help"), None)
    return jax.shard_map(
        per_device, mesh=mesh, in_specs=in_specs, out_specs=out_specs, check_vma=False
    )
```

```python
import functools

import jax
import jax.numpy as jnp
from jax import lax
from jax.experimental import pallas as pl
from jax.experimental.pallas import tpu as pltpu
from jax.sharding import PartitionSpec as P

HEADS = 32
KV_HEADS = 8
HEAD_DIM = 128
TILE = 64
NVERT = 24
NGROUP = 6
GROUP_HEADS = 4
TILES_LOCAL = 8
KEYS = NVERT * TILE
CHUNK = 256
CHUNK_TILES = CHUNK // TILE
NCHUNK = KEYS // CHUNK
ROWS = TILES_LOCAL * TILE
NEG = -1e30
HALF = ROWS // 2
BATCH = TILES_LOCAL // 2
MESH = pl.DeviceIdType.MESH
EXP_SCALE = HEAD_DIM ** -0.5 * 1.4426950408889634


def dot_t(a, b):
    return lax.dot_general(a, b, (((1,), (1,)), ((), ())), preferred_element_type=jnp.float32)


def make_bias(first_tile, plan, bias_v, bias_s):
    lane = lax.broadcasted_iota(jnp.int32, (TILES_LOCAL, 128), 1)
    tile = lax.broadcasted_iota(jnp.int32, (TILES_LOCAL, 128), 0) + first_tile
    slot_of = lax.broadcasted_iota(jnp.int32, (128, KEYS), 1) // TILE
    spread = jnp.where(slot_of == lax.broadcasted_iota(jnp.int32, (128, KEYS), 0), 1.0, 0.0).astype(jnp.bfloat16)
    for k in range(GROUP_HEADS):
        named = jnp.zeros((TILES_LOCAL, 128), jnp.int32)
        for n in range(2):
            mask = jnp.broadcast_to(plan[k, n:n + 1, :], (TILES_LOCAL, 128))
            named += jnp.where(lane + n * 128 == tile, mask, 0)
        named = jnp.sum(named, axis=1, keepdims=True)
        vert = jnp.broadcast_to(plan[k, 2:3, :], (TILES_LOCAL, 128))
        slash = jnp.broadcast_to(plan[k, 3:4, :], (TILES_LOCAL, 128))
        covered = jnp.zeros((TILES_LOCAL, 128), jnp.bool_)
        for n in range(NVERT):
            covered |= (tile - vert) == slash[:, n:n + 1]
        unit = lane // 8
        bit_v = lax.shift_right_logical(jnp.broadcast_to(named, unit.shape), jnp.minimum(unit, 2)) & 1
        bit_s = lax.shift_right_logical(jnp.broadcast_to(named, unit.shape), jnp.minimum(unit + 3, 5)) & 1
        real = lane < NVERT
        att_v = real & (vert <= tile) & jnp.logical_not(covered) & (bit_v == 1)
        att_s = real & (slash <= tile) & (bit_s == 1)
        for att, bias in ((att_v, bias_v), (att_s, bias_s)):
            hot = jnp.where(att, 1.0, 0.0).astype(jnp.bfloat16)
            wide = jnp.dot(hot, spread, preferred_element_type=jnp.float32)
            bias[k] = ((wide - 1.0) * (-NEG)).reshape(TILES_LOCAL, 1, KEYS)


def tile_of(ref, place):
    shard = lax.shift_right_logical(place, 3)
    row = (place & (TILES_LOCAL - 1)) * TILE
    return ref[shard, pl.ds(row, TILE), :]


def tiles_of(ref, places):
    return jnp.concatenate([tile_of(ref, p) for p in places], axis=0)


def score_vertical(k, q_ref, k_ref, slots, bias_v, score_v):
    for c in range(NCHUNK):
        keys = tiles_of(k_ref, [slots[k, 2, c * CHUNK_TILES + n] for n in range(CHUNK_TILES)])
        s = dot_t(q_ref[:, pl.ds(pl.multiple_of(k * HEAD_DIM, HEAD_DIM), HEAD_DIM)], keys)
        cols = slice(c * CHUNK, (c + 1) * CHUNK)
        s = s.reshape(TILES_LOCAL, TILE, CHUNK) + bias_v[k, :, :, cols]
        score_v[:, cols] = s.reshape(ROWS, CHUNK)


def score_tiles(k, tiles, first_tile, q_ref, k_ref, slots, bias_s, score_v, p_v, p_s, ell):
    row = lax.broadcasted_iota(jnp.int32, (TILE, CHUNK), 0)
    col = lax.broadcasted_iota(jnp.int32, (TILE, CHUNK), 1)
    diagonal = jnp.where((col < TILE) & (col > row), NEG, 0.0)
    for t in tiles:
        rows = pl.ds(pl.multiple_of(t * TILE, TILE), TILE)
        q = q_ref[rows, pl.ds(pl.multiple_of(k * HEAD_DIM, HEAD_DIM), HEAD_DIM)]
        parts = []
        for c in range(NCHUNK):
            places = [jnp.maximum(first_tile + t - slots[k, 3, c * CHUNK_TILES + n], 0) for n in range(CHUNK_TILES)]
            s = dot_t(q, tiles_of(k_ref, places))
            s = s + bias_s[k, t, :, c * CHUNK:(c + 1) * CHUNK]
            if c == 0:
                s = s + diagonal
            parts.append(s)
        for c in range(NCHUNK):
            parts.append(score_v[rows, c * CHUNK:(c + 1) * CHUNK])
        peak = functools.reduce(jnp.maximum, parts)
        peak = jnp.max(peak, axis=1, keepdims=True)
        total = jnp.zeros((TILE, CHUNK), jnp.float32)
        for c, s in enumerate(parts):
            p = jnp.exp2((s - peak) * EXP_SCALE)
            total += p
            out = p_s if c < NCHUNK else p_v
            cc = c % NCHUNK
            out[k, rows, cc * CHUNK:(cc + 1) * CHUNK] = p.astype(jnp.bfloat16)
        ell[k, rows, :] = jnp.broadcast_to(jnp.sum(total, axis=1, keepdims=True), (TILE, HEAD_DIM))


def value_head(k, first_tile, v_ref, slots, p_v, p_s, ell, acc, out_buf):
    values = tiles_of(v_ref, [slots[k, 2, n] for n in range(NVERT)])
    acc[...] = jnp.dot(p_v[k], values, preferred_element_type=jnp.float32)

    @pl.loop(0, TILES_LOCAL // BATCH)
    def _(batch):
        for n in range(BATCH):
            t = batch * BATCH + n
            rows = pl.ds(pl.multiple_of(t * TILE, TILE), TILE)
            places = [jnp.maximum(first_tile + t - slots[k, 3, n], 0) for n in range(NVERT)]
            o = jnp.dot(p_s[k, rows, :], tiles_of(v_ref, places), preferred_element_type=jnp.float32)
            out_buf[k, rows, :] = ((o + acc[rows, :]) / ell[k, rows, :]).astype(jnp.bfloat16)


class Gather:
    def __init__(self, me, z, buf, rows, send, recv):
        self.me, self.z, self.buf, self.rows, self.send, self.recv = me, z, buf, rows, send, recv
        self.core = me % 2
        x, y = me // 8, (me // 2) % 4
        c = self.core
        self.a = x * (1 - c) + y * c
        self.b = y * (1 - c) + x * c
        self.started = []

    def at(self, da, db):
        c = self.core
        a, b = (self.a + da) % 4, (self.b + db) % 4
        x = a * (1 - c) + b * c
        y = b * (1 - c) + a * c
        return (x * 4 + y) * 2 + c

    def sibling(self, shard):
        return shard + 1 - 2 * self.core

    def region(self, shard, half):
        if half is None:
            return self.buf.at[shard]
        if half == 0:
            return self.buf.at[shard, pl.ds(0, HALF)]
        return self.buf.at[shard, pl.ds(HALF, self.rows - HALF)]

    def copy(self, shard, half, target, n):
        region = self.region(shard, half)
        return pltpu.make_async_remote_copy(
            src_ref=region, dst_ref=region, send_sem=self.send.at[n],
            recv_sem=self.recv.at[shard, 0 if half is None else half],
            device_id=(target, self.z), device_id_type=MESH)

    def put(self, shard, half, target):
        copy = self.copy(shard, half, target, len(self.started))
        copy.start()
        self.started.append(half)

    def got(self, shard, half):
        self.copy(shard, half, self.sibling(self.me), 0).wait_recv()

    def put_a(self, shard, half, da):
        self.put(shard, half, self.at(da, 0))

    def put_b(self, shard, half, way=None):
        for db in (1, -1) if way is None else (way,):
            self.put(shard, half, self.at(0, db))

    def across(self, shard):
        self.put(shard, None, self.sibling(self.me))

    def own(self, half):
        mine = self.me
        self.put_a(mine, half, 1)
        self.put_a(mine, half, -1)
        self.put_b(mine, half)

    def first(self):
        left, right = self.at(-1, 0), self.at(1, 0)
        self.got(left, 0)
        self.put_a(left, 0, 1)
        self.got(right, 0)
        self.got(right, 1)
        self.put_a(right, 1, -1)
        self.got(left, 1)
        for shard in (left, right):
            for half in (0, 1):
                self.put_b(shard, half)
            self.across(shard)

    def second(self):
        far = self.at(2, 0)
        for half in (0, 1):
            self.got(far, half)
            self.put_b(far, half)
        self.across(far)

    def third(self, da):
        down, up = self.at(da, -1), self.at(da, 1)
        self.got(down, 0)
        self.put_b(down, 0, 1)
        self.got(up, 0)
        self.got(up, 1)
        self.put_b(up, 1, -1)
        self.got(down, 1)
        self.across(down)
        self.across(up)

    def fourth(self, da):
        far = self.at(da, 2)
        self.got(far, 0)
        self.got(far, 1)
        self.across(far)

    def stages(self):
        return [
            self.first, lambda: self.third(0), self.second, lambda: self.third(-1), lambda: self.fourth(0),
            lambda: self.third(1), lambda: self.fourth(-1), lambda: self.third(2), lambda: self.fourth(1),
            lambda: self.fourth(2),
        ]

    def last(self):
        for da in range(4):
            for db in range(4):
                self.got(self.sibling(self.at(da, db)), None)

    def drain(self):
        for n, half in enumerate(self.started):
            self.copy(self.me, half, self.sibling(self.me), n).wait_send()


N_SENDS = 46
N_SEQ = 32


def fused_kernel(q_hbm, kv_hbm, verts_ref, slashes_ref, codes_ref, out_ref,
                 k_buf, v_buf, q_ref, parts, plan, slots, bias_v, bias_s, score_v, p_v, p_s, ell, acc, out_buf,
                 local_sem, part_send, part_recv, plan_send, plan_recv, k_send, k_recv, v_send, v_recv, out_send, out_recv):
    me = lax.axis_index("seq")
    z = lax.axis_index("help")
    keys = Gather(me, z, k_buf, ROWS, k_send, k_recv)
    values = Gather(me, z, v_buf, ROWS, v_send, v_recv)
    first_tile = me * TILES_LOCAL
    owner = me // GROUP_HEADS

    barrier = pltpu.get_barrier_semaphore()
    peers = [(keys.at(1, 0), z), (keys.at(-1, 0), z), (keys.at(0, 1), z), (keys.at(0, -1), z), (keys.sibling(me), z)]
    peers += [(me, (z + n) % 8) for n in range(1, 8)]
    for peer in peers:
        pl.semaphore_signal(barrier, inc=1, device_id=peer, device_id_type=MESH)
    for k in range(GROUP_HEADS):
        @pl.when(me != z * GROUP_HEADS + k)
        def _():
            pl.semaphore_signal(barrier, inc=1, device_id=(z * GROUP_HEADS + k, z), device_id_type=MESH)

    k_cols = pl.ds(pl.multiple_of(z * HEAD_DIM, HEAD_DIM), HEAD_DIM)
    v_cols = pl.ds(pl.multiple_of(z * HEAD_DIM + KV_HEADS * HEAD_DIM, HEAD_DIM), HEAD_DIM)
    q_cols = pl.ds(pl.multiple_of(z * GROUP_HEADS * HEAD_DIM, GROUP_HEADS * HEAD_DIM), GROUP_HEADS * HEAD_DIM)
    k_local = pltpu.make_async_copy(kv_hbm.at[:, k_cols], k_buf.at[me, pl.ds(0, ROWS)], local_sem.at[0])
    v_local = pltpu.make_async_copy(kv_hbm.at[:, v_cols], v_buf.at[me], local_sem.at[1])
    q_local = pltpu.make_async_copy(q_hbm.at[:, q_cols], q_ref, local_sem.at[2])
    k_local.start()
    v_local.start()
    q_local.start()

    width = codes_ref.shape[1]
    tile = lax.broadcasted_iota(jnp.int32, (128, width), 0)
    eye = lax.broadcasted_iota(jnp.int32, (128, 128), 0) == lax.broadcasted_iota(jnp.int32, (128, 128), 1)
    named = []
    for n in range(2):
        group = jnp.broadcast_to(codes_ref[...], (128, width)) - (tile + n * 128) * NGROUP
        bits = jnp.where((group >= 0) & (group < NGROUP), lax.shift_left(1, jnp.clip(group, 0, NGROUP - 1)), 0)
        column = jnp.sum(bits, axis=1, keepdims=True)
        named.append(jnp.sum(jnp.where(eye, jnp.broadcast_to(column, (128, 128)), 0), axis=0, keepdims=True))
    parts[z] = jnp.concatenate(named + [jnp.zeros((6, 128), jnp.int32)], axis=0)

    @pl.when(z != owner)
    def _():
        pl.semaphore_wait(barrier, len(peers))

    @pl.when(z == owner)
    def _():
        pl.semaphore_wait(barrier, len(peers) + N_SEQ - 1)

    part = pltpu.make_async_remote_copy(
        src_ref=parts.at[z], dst_ref=parts.at[z], send_sem=part_send, recv_sem=part_recv.at[z],
        device_id=(me, owner), device_id_type=MESH)

    @pl.when(z != owner)
    def _():
        part.start()

    k_local.wait()
    keys.own(0)
    keys.own(1)
    keys.across(me)
    mine = me % GROUP_HEADS

    def plan_copy(k, n):
        return pltpu.make_async_remote_copy(
            src_ref=plan.at[k], dst_ref=plan.at[k], send_sem=plan_send.at[n], recv_sem=plan_recv.at[k],
            device_id=((me + n) % N_SEQ, z), device_id_type=MESH)

    @pl.when(z != owner)
    def _():
        part.wait_send()

    @pl.when(z == owner)
    def _():
        for n in range(1, 8):
            other = (z + n) % 8
            pltpu.make_async_remote_copy(
                src_ref=parts.at[other], dst_ref=parts.at[other], send_sem=part_send, recv_sem=part_recv.at[other],
                device_id=(me, other), device_id_type=MESH).wait_recv()
        total = parts[0]
        for n in range(1, 8):
            total += parts[n]
        plan[mine] = total
        plan[mine, 2:3, 0:NVERT] = verts_ref[...]
        plan[mine, 3:4, 0:NVERT] = slashes_ref[...]
        for n in range(1, N_SEQ):
            plan_copy(mine, n).start()

    stages = keys.stages()
    for stage in stages[:4]:
        stage()
    for k in range(GROUP_HEADS):
        @pl.when(me != z * GROUP_HEADS + k)
        def _():
            plan_copy(k, 1).wait_recv()
    slots_copy = pltpu.make_async_copy(plan, slots, local_sem.at[3])
    slots_copy.start()
    for stage in stages[4:8]:
        stage()
    v_local.wait()
    values.own(0)
    values.own(1)
    values.across(me)
    make_bias(first_tile, plan, bias_v, bias_s)
    for stage in stages[8:]:
        stage()
    slots_copy.wait()
    q_local.wait()
    keys.last()

    stages = values.stages()
    gaps = [stages[:1], stages[1:3], stages[3:4], stages[4:6], stages[6:8], stages[8:9], stages[9:], []]

    @pl.loop(0, GROUP_HEADS)
    def _(k):
        score_vertical(k, q_ref, k_buf, slots, bias_v, score_v)

        @pl.loop(0, TILES_LOCAL // BATCH)
        def _(batch):
            tiles = [batch * BATCH + n for n in range(BATCH)]
            score_tiles(k, tiles, first_tile, q_ref, k_buf, slots, bias_s, score_v, p_v, p_s, ell)
            for n, gap in enumerate(gaps):
                @pl.when(k * (TILES_LOCAL // BATCH) + batch == n)
                def _():
                    for stage in gap:
                        stage()

    values.last()

    def out_copy(k, n):
        other = (z + n) % 8
        return pltpu.make_async_remote_copy(
            src_ref=out_buf.at[k, pl.ds(pl.multiple_of(other * TILE, TILE), TILE)],
            dst_ref=out_ref.at[:, pl.ds(pl.multiple_of((z * GROUP_HEADS + k) * HEAD_DIM, HEAD_DIM), HEAD_DIM)],
            send_sem=out_send.at[k, n], recv_sem=out_recv.at[z, k], device_id=(me, other), device_id_type=MESH)

    @pl.loop(0, GROUP_HEADS)
    def _(k):
        value_head(k, first_tile, v_buf, slots, p_v, p_s, ell, acc, out_buf)
        for n in range(1, 8):
            out_copy(k, n).start()
        cols = pl.ds(pl.multiple_of((z * GROUP_HEADS + k) * HEAD_DIM, HEAD_DIM), HEAD_DIM)
        out_ref[:, cols] = out_buf[k, pl.ds(pl.multiple_of(z * TILE, TILE), TILE), :]

    @pl.loop(0, GROUP_HEADS)
    def _(k):
        for n in range(1, 8):
            other = (z + n) % 8
            cols = pl.ds(pl.multiple_of((other * GROUP_HEADS + k) * HEAD_DIM, HEAD_DIM), HEAD_DIM)
            pltpu.make_async_remote_copy(
                src_ref=out_buf.at[k, pl.ds(0, TILE)], dst_ref=out_ref.at[:, cols],
                send_sem=out_send.at[k, n], recv_sem=out_recv.at[other, k], device_id=(me, other),
                device_id_type=MESH).wait_recv()
            out_copy(k, n).wait_send()

    keys.drain()
    values.drain()

    @pl.when(z == owner)
    def _():
        for n in range(1, N_SEQ):
            plan_copy(mine, n).wait_send()


def per_device(queries, keys_values, verticals, slashes, units):
    vmem = pl.BlockSpec(memory_space=pltpu.VMEM)
    hbm = pl.BlockSpec(memory_space=pl.ANY)
    dma = pltpu.SemaphoreType.DMA
    seq = lax.axis_size("seq")
    return pl.pallas_call(
        fused_kernel,
        out_shape=jax.ShapeDtypeStruct((TILE, HEADS * HEAD_DIM), jnp.bfloat16),
        in_specs=[hbm, hbm, vmem, vmem, vmem],
        out_specs=vmem,
        scratch_shapes=[
            pltpu.VMEM((seq, ROWS, HEAD_DIM), jnp.bfloat16),
            pltpu.VMEM((seq, ROWS, HEAD_DIM), jnp.bfloat16),
            pltpu.VMEM((ROWS, GROUP_HEADS * HEAD_DIM), jnp.bfloat16),
            pltpu.VMEM((8, 8, 128), jnp.int32),
            pltpu.VMEM((GROUP_HEADS, 8, 128), jnp.int32),
            pltpu.SMEM((GROUP_HEADS, 8, 128), jnp.int32),
            pltpu.VMEM((GROUP_HEADS, TILES_LOCAL, 1, KEYS), jnp.float32),
            pltpu.VMEM((GROUP_HEADS, TILES_LOCAL, 1, KEYS), jnp.float32),
            pltpu.VMEM((ROWS, KEYS), jnp.float32),
            pltpu.VMEM((GROUP_HEADS, ROWS, KEYS), jnp.bfloat16),
            pltpu.VMEM((GROUP_HEADS, ROWS, KEYS), jnp.bfloat16),
            pltpu.VMEM((GROUP_HEADS, ROWS, HEAD_DIM), jnp.float32),
            pltpu.VMEM((ROWS, HEAD_DIM), jnp.float32),
            pltpu.VMEM((GROUP_HEADS, ROWS, HEAD_DIM), jnp.bfloat16),
            dma((4,)), dma, dma((8,)), dma((N_SEQ,)), dma((GROUP_HEADS,)),
            dma((N_SENDS,)), dma((seq, 2)), dma((N_SENDS,)), dma((seq, 2)),
            dma((GROUP_HEADS, 8)), dma((8, GROUP_HEADS)),
        ],
        compiler_params=pltpu.CompilerParams(
            vmem_limit_bytes=56 * 1024 * 1024, collective_id=0, has_side_effects=True),
        name="fused_attention",
    )(queries, keys_values, verticals, slashes, units[0])


def solution(mesh):
    in_specs = (
        P("seq", None),
        P("seq", None),
        P("seq", None),
        P("seq", None),
        P("seq", "help", None),
    )
    out_specs = P(("seq", "help"), None)
    return jax.shard_map(
        per_device, mesh=mesh, in_specs=in_specs, out_specs=out_specs, check_vma=False
    )
```

```python
import functools

import jax
import jax.numpy as jnp
from jax import lax
from jax.experimental import pallas as pl
from jax.experimental.pallas import tpu as pltpu
from jax.sharding import PartitionSpec as P

HEADS = 32
KV_HEADS = 8
HEAD_DIM = 128
TILE = 64
NVERT = 24
NGROUP = 6
GROUP_HEADS = 4
TILES_LOCAL = 8
KEYS = NVERT * TILE
CHUNK = 256
CHUNK_TILES = CHUNK // TILE
NCHUNK = KEYS // CHUNK
ROWS = TILES_LOCAL * TILE
NEG = -1e30
HALF = ROWS // 2
BATCH = TILES_LOCAL // 2
MESH = pl.DeviceIdType.MESH
EXP_SCALE = HEAD_DIM ** -0.5 * 1.4426950408889634


def dot_t(a, b):
    return lax.dot_general(a, b, (((1,), (1,)), ((), ())), preferred_element_type=jnp.float32)


def make_bias(first_tile, plan, bias_v, bias_s):
    lane = lax.broadcasted_iota(jnp.int32, (TILES_LOCAL, 128), 1)
    tile = lax.broadcasted_iota(jnp.int32, (TILES_LOCAL, 128), 0) + first_tile
    slot_of = lax.broadcasted_iota(jnp.int32, (128, KEYS), 1) // TILE
    spread = jnp.where(slot_of == lax.broadcasted_iota(jnp.int32, (128, KEYS), 0), 1.0, 0.0).astype(jnp.bfloat16)
    for k in range(GROUP_HEADS):
        named = jnp.zeros((TILES_LOCAL, 128), jnp.int32)
        for n in range(2):
            mask = jnp.broadcast_to(plan[k, n:n + 1, :], (TILES_LOCAL, 128))
            named += jnp.where(lane + n * 128 == tile, mask, 0)
        named = jnp.sum(named, axis=1, keepdims=True)
        vert = jnp.broadcast_to(plan[k, 2:3, :], (TILES_LOCAL, 128))
        slash = jnp.broadcast_to(plan[k, 3:4, :], (TILES_LOCAL, 128))
        covered = jnp.zeros((TILES_LOCAL, 128), jnp.bool_)
        for n in range(NVERT):
            covered |= (tile - vert) == slash[:, n:n + 1]
        unit = lane // 8
        bit_v = lax.shift_right_logical(jnp.broadcast_to(named, unit.shape), jnp.minimum(unit, 2)) & 1
        bit_s = lax.shift_right_logical(jnp.broadcast_to(named, unit.shape), jnp.minimum(unit + 3, 5)) & 1
        real = lane < NVERT
        att_v = real & (vert <= tile) & jnp.logical_not(covered) & (bit_v == 1)
        att_s = real & (slash <= tile) & (bit_s == 1)
        for att, bias in ((att_v, bias_v), (att_s, bias_s)):
            hot = jnp.where(att, 1.0, 0.0).astype(jnp.bfloat16)
            wide = jnp.dot(hot, spread, preferred_element_type=jnp.float32)
            bias[k] = ((wide - 1.0) * (-NEG)).reshape(TILES_LOCAL, 1, KEYS)


def tile_of(ref, place):
    shard = lax.shift_right_logical(place, 3)
    row = (place & (TILES_LOCAL - 1)) * TILE
    return ref[shard, pl.ds(row, TILE), :]


def tiles_of(ref, places):
    return jnp.concatenate([tile_of(ref, p) for p in places], axis=0)


def score_vertical(k, q_ref, k_ref, slots, bias_v, score_v):
    for c in range(NCHUNK):
        keys = tiles_of(k_ref, [slots[k, 2, c * CHUNK_TILES + n] for n in range(CHUNK_TILES)])
        s = dot_t(q_ref[:, pl.ds(pl.multiple_of(k * HEAD_DIM, HEAD_DIM), HEAD_DIM)], keys)
        cols = slice(c * CHUNK, (c + 1) * CHUNK)
        s = s.reshape(TILES_LOCAL, TILE, CHUNK) + bias_v[k, :, :, cols]
        score_v[:, cols] = s.reshape(ROWS, CHUNK)


def score_tiles(k, tiles, first_tile, q_ref, k_ref, slots, bias_s, score_v, p_v, p_s, ell):
    row = lax.broadcasted_iota(jnp.int32, (TILE, CHUNK), 0)
    col = lax.broadcasted_iota(jnp.int32, (TILE, CHUNK), 1)
    diagonal = jnp.where((col < TILE) & (col > row), NEG, 0.0)
    for t in tiles:
        rows = pl.ds(pl.multiple_of(t * TILE, TILE), TILE)
        q = q_ref[rows, pl.ds(pl.multiple_of(k * HEAD_DIM, HEAD_DIM), HEAD_DIM)]
        parts = []
        for c in range(NCHUNK):
            places = [jnp.maximum(first_tile + t - slots[k, 3, c * CHUNK_TILES + n], 0) for n in range(CHUNK_TILES)]
            s = dot_t(q, tiles_of(k_ref, places))
            s = s + bias_s[k, t, :, c * CHUNK:(c + 1) * CHUNK]
            if c == 0:
                s = s + diagonal
            parts.append(s)
        for c in range(NCHUNK):
            parts.append(score_v[rows, c * CHUNK:(c + 1) * CHUNK])
        peak = functools.reduce(jnp.maximum, parts)
        peak = jnp.max(peak, axis=1, keepdims=True)
        total = jnp.zeros((TILE, CHUNK), jnp.float32)
        for c, s in enumerate(parts):
            p = jnp.exp2((s - peak) * EXP_SCALE)
            total += p
            out = p_s if c < NCHUNK else p_v
            cc = c % NCHUNK
            out[k, rows, cc * CHUNK:(cc + 1) * CHUNK] = p.astype(jnp.bfloat16)
        ell[k, rows, :] = jnp.broadcast_to(jnp.sum(total, axis=1, keepdims=True), (TILE, HEAD_DIM))


def value_head(k, first_tile, v_ref, slots, p_v, p_s, ell, acc, out_buf):
    values = tiles_of(v_ref, [slots[k, 2, n] for n in range(NVERT)])
    acc[...] = jnp.dot(p_v[k], values, preferred_element_type=jnp.float32)

    @pl.loop(0, TILES_LOCAL // BATCH)
    def _(batch):
        for n in range(BATCH):
            t = batch * BATCH + n
            rows = pl.ds(pl.multiple_of(t * TILE, TILE), TILE)
            places = [jnp.maximum(first_tile + t - slots[k, 3, n], 0) for n in range(NVERT)]
            o = jnp.dot(p_s[k, rows, :], tiles_of(v_ref, places), preferred_element_type=jnp.float32)
            out_buf[k, rows, :] = ((o + acc[rows, :]) / ell[k, rows, :]).astype(jnp.bfloat16)


class Gather:
    def __init__(self, me, z, buf, rows, send, recv):
        self.me, self.z, self.buf, self.rows, self.send, self.recv = me, z, buf, rows, send, recv
        self.core = me % 2
        x, y = me // 8, (me // 2) % 4
        c = self.core
        self.a = x * (1 - c) + y * c
        self.b = y * (1 - c) + x * c
        self.started = []

    def at(self, da, db):
        c = self.core
        a, b = (self.a + da) % 4, (self.b + db) % 4
        x = a * (1 - c) + b * c
        y = b * (1 - c) + a * c
        return (x * 4 + y) * 2 + c

    def sibling(self, shard):
        return shard + 1 - 2 * self.core

    def region(self, shard, half):
        if half is None:
            return self.buf.at[shard]
        if half == 0:
            return self.buf.at[shard, pl.ds(0, HALF)]
        return self.buf.at[shard, pl.ds(HALF, self.rows - HALF)]

    def copy(self, shard, half, target, n):
        region = self.region(shard, half)
        return pltpu.make_async_remote_copy(
            src_ref=region, dst_ref=region, send_sem=self.send.at[n],
            recv_sem=self.recv.at[shard, 0 if half is None else half],
            device_id=(target, self.z), device_id_type=MESH)

    def put(self, shard, half, target):
        copy = self.copy(shard, half, target, len(self.started))
        copy.start()
        self.started.append(half)

    def got(self, shard, half):
        self.copy(shard, half, self.sibling(self.me), 0).wait_recv()

    def put_a(self, shard, half, ways):
        for da in ways:
            self.put(shard, half, self.at(da, 0))

    def put_b(self, shard, half, ways):
        for db in ways:
            self.put(shard, half, self.at(0, db))

    def across(self, shard):
        self.put(shard, None, self.sibling(self.me))

    def own(self):
        for half in (0, 1):
            self.put_a(self.me, half, (1, -1))
            self.put_b(self.me, half, (1, -1))
        for half in (0, 1):
            self.put_a(self.me, half, (2,))
        self.across(self.me)

    def near(self, da):
        shard = self.at(da, 0)
        for half in (0, 1):
            self.got(shard, half)
            self.put_b(shard, half, (1, -1))
        if da == 2:
            for half in (0, 1):
                self.put_b(shard, half, (2,))
        self.across(shard)

    def pass_on(self, da):
        down, up = self.at(da, -1), self.at(da, 1)
        self.got(down, 0)
        if da != 2:
            self.put_b(down, 0, (1,))
        self.got(up, 0)
        self.got(up, 1)
        if da != 2:
            self.put_b(up, 1, (-1,))
        self.got(down, 1)
        self.across(down)
        self.across(up)

    def far(self, da):
        shard = self.at(da, 2)
        self.got(shard, 0)
        self.got(shard, 1)
        self.across(shard)

    def sends(self):
        self.near(-1)
        self.near(1)
        self.pass_on(0)
        self.near(2)
        self.pass_on(-1)
        self.pass_on(1)

    def ends(self):
        self.far(0)
        self.pass_on(2)
        self.far(-1)
        self.far(1)
        self.far(2)

    def last(self):
        for da in range(4):
            for db in range(4):
                self.got(self.sibling(self.at(da, db)), None)

    def drain(self):
        for n, half in enumerate(self.started):
            self.copy(self.me, half, self.sibling(self.me), n).wait_send()


N_SENDS = 49
N_SEQ = 32


def fused_kernel(q_hbm, kv_hbm, verts_ref, slashes_ref, codes_ref, out_ref,
                 k_buf, v_buf, q_ref, parts, plan, slots, bias_v, bias_s, score_v, p_v, p_s, ell, acc, out_buf,
                 local_sem, part_send, part_recv, plan_send, plan_recv, k_send, k_recv, v_send, v_recv, out_send, out_recv):
    me = lax.axis_index("seq")
    z = lax.axis_index("help")
    keys = Gather(me, z, k_buf, ROWS, k_send, k_recv)
    values = Gather(me, z, v_buf, ROWS, v_send, v_recv)
    first_tile = me * TILES_LOCAL
    owner = me // GROUP_HEADS

    barrier = pltpu.get_barrier_semaphore()
    peers = [(keys.at(n, 0), z) for n in (1, 2, 3)] + [(keys.at(0, n), z) for n in (1, 2, 3)] + [(keys.sibling(me), z)]
    peers += [(me, (z + n) % 8) for n in range(1, 8)]
    for peer in peers:
        pl.semaphore_signal(barrier, inc=1, device_id=peer, device_id_type=MESH)
    for k in range(GROUP_HEADS):
        @pl.when(me != z * GROUP_HEADS + k)
        def _():
            pl.semaphore_signal(barrier, inc=1, device_id=(z * GROUP_HEADS + k, z), device_id_type=MESH)

    k_cols = pl.ds(pl.multiple_of(z * HEAD_DIM, HEAD_DIM), HEAD_DIM)
    v_cols = pl.ds(pl.multiple_of(z * HEAD_DIM + KV_HEADS * HEAD_DIM, HEAD_DIM), HEAD_DIM)
    q_cols = pl.ds(pl.multiple_of(z * GROUP_HEADS * HEAD_DIM, GROUP_HEADS * HEAD_DIM), GROUP_HEADS * HEAD_DIM)
    k_local = pltpu.make_async_copy(kv_hbm.at[:, k_cols], k_buf.at[me, pl.ds(0, ROWS)], local_sem.at[0])
    v_local = pltpu.make_async_copy(kv_hbm.at[:, v_cols], v_buf.at[me], local_sem.at[1])
    q_local = pltpu.make_async_copy(q_hbm.at[:, q_cols], q_ref, local_sem.at[2])
    k_local.start()
    v_local.start()
    q_local.start()

    width = codes_ref.shape[1]
    tile = lax.broadcasted_iota(jnp.int32, (128, width), 0)
    eye = lax.broadcasted_iota(jnp.int32, (128, 128), 0) == lax.broadcasted_iota(jnp.int32, (128, 128), 1)
    named = []
    for n in range(2):
        group = jnp.broadcast_to(codes_ref[...], (128, width)) - (tile + n * 128) * NGROUP
        bits = jnp.where((group >= 0) & (group < NGROUP), lax.shift_left(1, jnp.clip(group, 0, NGROUP - 1)), 0)
        column = jnp.sum(bits, axis=1, keepdims=True)
        named.append(jnp.sum(jnp.where(eye, jnp.broadcast_to(column, (128, 128)), 0), axis=0, keepdims=True))
    parts[z] = jnp.concatenate(named + [jnp.zeros((6, 128), jnp.int32)], axis=0)

    @pl.when(z != owner)
    def _():
        pl.semaphore_wait(barrier, len(peers))

    @pl.when(z == owner)
    def _():
        pl.semaphore_wait(barrier, len(peers) + N_SEQ - 1)

    part = pltpu.make_async_remote_copy(
        src_ref=parts.at[z], dst_ref=parts.at[z], send_sem=part_send, recv_sem=part_recv.at[z],
        device_id=(me, owner), device_id_type=MESH)

    @pl.when(z != owner)
    def _():
        part.start()

    k_local.wait()
    keys.own()
    mine = me % GROUP_HEADS

    def plan_copy(k, n):
        return pltpu.make_async_remote_copy(
            src_ref=plan.at[k], dst_ref=plan.at[k], send_sem=plan_send.at[n], recv_sem=plan_recv.at[k],
            device_id=((me + n) % N_SEQ, z), device_id_type=MESH)

    @pl.when(z != owner)
    def _():
        part.wait_send()

    @pl.when(z == owner)
    def _():
        for n in range(1, 8):
            other = (z + n) % 8
            pltpu.make_async_remote_copy(
                src_ref=parts.at[other], dst_ref=parts.at[other], send_sem=part_send, recv_sem=part_recv.at[other],
                device_id=(me, other), device_id_type=MESH).wait_recv()
        total = parts[0]
        for n in range(1, 8):
            total += parts[n]
        plan[mine] = total
        plan[mine, 2:3, 0:NVERT] = verts_ref[...]
        plan[mine, 3:4, 0:NVERT] = slashes_ref[...]
        for n in range(1, N_SEQ):
            plan_copy(mine, n).start()

    keys.sends()
    v_local.wait()
    values.own()
    for k in range(GROUP_HEADS):
        @pl.when(me != z * GROUP_HEADS + k)
        def _():
            plan_copy(k, 1).wait_recv()
    slots_copy = pltpu.make_async_copy(plan, slots, local_sem.at[3])
    slots_copy.start()
    make_bias(first_tile, plan, bias_v, bias_s)
    keys.ends()
    slots_copy.wait()
    q_local.wait()
    keys.last()

    def gap(n):
        if n == 0:
            values.near(-1)
            values.near(1)
        elif n == 1:
            values.pass_on(0)
            values.near(2)
        elif n == 3:
            values.pass_on(-1)
            values.pass_on(1)
        elif n == 4:
            keys.drain()
        elif n == 5:
            values.ends()
            values.last()

    def out_copy(k, n):
        other = (z + n) % 8
        return pltpu.make_async_remote_copy(
            src_ref=out_buf.at[k, pl.ds(pl.multiple_of(other * TILE, TILE), TILE)],
            dst_ref=out_ref.at[:, pl.ds(pl.multiple_of((z * GROUP_HEADS + k) * HEAD_DIM, HEAD_DIM), HEAD_DIM)],
            send_sem=out_send.at[k, n], recv_sem=out_recv.at[z, k], device_id=(me, other), device_id_type=MESH)

    @pl.loop(0, 2 * GROUP_HEADS)
    def _(step):
        @pl.when((step < 3) | (step == 6))
        def _():
            k = step - 3 * (step // 6)
            score_vertical(k, q_ref, k_buf, slots, bias_v, score_v)

            @pl.loop(0, TILES_LOCAL // BATCH)
            def _(batch):
                tiles = [batch * BATCH + n for n in range(BATCH)]
                score_tiles(k, tiles, first_tile, q_ref, k_buf, slots, bias_s, score_v, p_v, p_s, ell)
                for n in (0, 1, 3, 4, 5):
                    @pl.when(k * (TILES_LOCAL // BATCH) + batch == n)
                    def _():
                        gap(n)

        @pl.when(((step > 2) & (step < 6)) | (step == 7))
        def _():
            k = step - 3 - step // 7
            value_head(k, first_tile, v_buf, slots, p_v, p_s, ell, acc, out_buf)
            for n in range(1, 8):
                out_copy(k, n).start()
            cols = pl.ds(pl.multiple_of((z * GROUP_HEADS + k) * HEAD_DIM, HEAD_DIM), HEAD_DIM)
            out_ref[:, cols] = out_buf[k, pl.ds(pl.multiple_of(z * TILE, TILE), TILE), :]

    values.drain()

    @pl.when(z == owner)
    def _():
        for n in range(1, N_SEQ):
            plan_copy(mine, n).wait_send()

    @pl.loop(0, GROUP_HEADS)
    def _(k):
        for n in range(1, 8):
            other = (z + n) % 8
            cols = pl.ds(pl.multiple_of((other * GROUP_HEADS + k) * HEAD_DIM, HEAD_DIM), HEAD_DIM)
            pltpu.make_async_remote_copy(
                src_ref=out_buf.at[k, pl.ds(0, TILE)], dst_ref=out_ref.at[:, cols],
                send_sem=out_send.at[k, n], recv_sem=out_recv.at[other, k], device_id=(me, other),
                device_id_type=MESH).wait_recv()
            out_copy(k, n).wait_send()


def per_device(queries, keys_values, verticals, slashes, units):
    vmem = pl.BlockSpec(memory_space=pltpu.VMEM)
    hbm = pl.BlockSpec(memory_space=pl.ANY)
    dma = pltpu.SemaphoreType.DMA
    seq = lax.axis_size("seq")
    return pl.pallas_call(
        fused_kernel,
        out_shape=jax.ShapeDtypeStruct((TILE, HEADS * HEAD_DIM), jnp.bfloat16),
        in_specs=[hbm, hbm, vmem, vmem, vmem],
        out_specs=vmem,
        scratch_shapes=[
            pltpu.VMEM((seq, ROWS, HEAD_DIM), jnp.bfloat16),
            pltpu.VMEM((seq, ROWS, HEAD_DIM), jnp.bfloat16),
            pltpu.VMEM((ROWS, GROUP_HEADS * HEAD_DIM), jnp.bfloat16),
            pltpu.VMEM((8, 8, 128), jnp.int32),
            pltpu.VMEM((GROUP_HEADS, 8, 128), jnp.int32),
            pltpu.SMEM((GROUP_HEADS, 8, 128), jnp.int32),
            pltpu.VMEM((GROUP_HEADS, TILES_LOCAL, 1, KEYS), jnp.float32),
            pltpu.VMEM((GROUP_HEADS, TILES_LOCAL, 1, KEYS), jnp.float32),
            pltpu.VMEM((ROWS, KEYS), jnp.float32),
            pltpu.VMEM((GROUP_HEADS, ROWS, KEYS), jnp.bfloat16),
            pltpu.VMEM((GROUP_HEADS, ROWS, KEYS), jnp.bfloat16),
            pltpu.VMEM((GROUP_HEADS, ROWS, HEAD_DIM), jnp.float32),
            pltpu.VMEM((ROWS, HEAD_DIM), jnp.float32),
            pltpu.VMEM((GROUP_HEADS, ROWS, HEAD_DIM), jnp.bfloat16),
            dma((4,)), dma, dma((8,)), dma((N_SEQ,)), dma((GROUP_HEADS,)),
            dma((N_SENDS,)), dma((seq, 2)), dma((N_SENDS,)), dma((seq, 2)),
            dma((GROUP_HEADS, 8)), dma((8, GROUP_HEADS)),
        ],
        compiler_params=pltpu.CompilerParams(
            vmem_limit_bytes=56 * 1024 * 1024, collective_id=0, has_side_effects=True),
        name="fused_attention",
    )(queries, keys_values, verticals, slashes, units[0])


def solution(mesh):
    in_specs = (
        P("seq", None),
        P("seq", None),
        P("seq", None),
        P("seq", None),
        P("seq", "help", None),
    )
    out_specs = P(("seq", "help"), None)
    return jax.shard_map(
        per_device, mesh=mesh, in_specs=in_specs, out_specs=out_specs, check_vma=False
    )
```

```python
import functools

import jax
import jax.numpy as jnp
from jax import lax
from jax.experimental import pallas as pl
from jax.experimental.pallas import tpu as pltpu
from jax.sharding import PartitionSpec as P

HEADS = 32
KV_HEADS = 8
HEAD_DIM = 128
TILE = 64
NVERT = 24
NGROUP = 6
GROUP_HEADS = 4
TILES_LOCAL = 8
KEYS = NVERT * TILE
CHUNK = 256
CHUNK_TILES = CHUNK // TILE
NCHUNK = KEYS // CHUNK
ROWS = TILES_LOCAL * TILE
NEG = -1e30
HALF = ROWS // 2
BATCH = TILES_LOCAL // 2
MESH = pl.DeviceIdType.MESH
EXP_SCALE = HEAD_DIM ** -0.5 * 1.4426950408889634


def dot_t(a, b):
    return lax.dot_general(a, b, (((1,), (1,)), ((), ())), preferred_element_type=jnp.float32)


def make_bias(first_tile, plan, bias_v, bias_s):
    lane = lax.broadcasted_iota(jnp.int32, (TILES_LOCAL, 128), 1)
    tile = lax.broadcasted_iota(jnp.int32, (TILES_LOCAL, 128), 0) + first_tile
    slot_of = lax.broadcasted_iota(jnp.int32, (128, KEYS), 1) // TILE
    spread = jnp.where(slot_of == lax.broadcasted_iota(jnp.int32, (128, KEYS), 0), 1.0, 0.0).astype(jnp.bfloat16)
    for k in range(GROUP_HEADS):
        named = jnp.zeros((TILES_LOCAL, 128), jnp.int32)
        for n in range(2):
            mask = jnp.broadcast_to(plan[k, n:n + 1, :], (TILES_LOCAL, 128))
            named += jnp.where(lane + n * 128 == tile, mask, 0)
        named = jnp.sum(named, axis=1, keepdims=True)
        vert = jnp.broadcast_to(plan[k, 2:3, :], (TILES_LOCAL, 128))
        slash = jnp.broadcast_to(plan[k, 3:4, :], (TILES_LOCAL, 128))
        covered = jnp.zeros((TILES_LOCAL, 128), jnp.bool_)
        for n in range(NVERT):
            covered |= (tile - vert) == slash[:, n:n + 1]
        unit = lane // 8
        bit_v = lax.shift_right_logical(jnp.broadcast_to(named, unit.shape), jnp.minimum(unit, 2)) & 1
        bit_s = lax.shift_right_logical(jnp.broadcast_to(named, unit.shape), jnp.minimum(unit + 3, 5)) & 1
        real = lane < NVERT
        att_v = real & (vert <= tile) & jnp.logical_not(covered) & (bit_v == 1)
        att_s = real & (slash <= tile) & (bit_s == 1)
        for att, bias in ((att_v, bias_v), (att_s, bias_s)):
            hot = jnp.where(att, 1.0, 0.0).astype(jnp.bfloat16)
            wide = jnp.dot(hot, spread, preferred_element_type=jnp.float32)
            bias[k] = ((wide - 1.0) * (-NEG)).reshape(TILES_LOCAL, 1, KEYS)


def tile_of(ref, place):
    shard = lax.shift_right_logical(place, 3)
    row = (place & (TILES_LOCAL - 1)) * TILE
    return ref[shard, pl.ds(row, TILE), :]


def tiles_of(ref, places):
    return jnp.concatenate([tile_of(ref, p) for p in places], axis=0)


def score_vertical(k, first_tile, q_ref, k_ref, slots, bias_v, score_v):
    for c in range(NCHUNK):
        places = [slots[k, 2, c * CHUNK_TILES + n] for n in range(CHUNK_TILES)]
        keys = tiles_of(k_ref, [jnp.minimum(p, first_tile + TILES_LOCAL - 1) for p in places])
        s = dot_t(q_ref[:, pl.ds(pl.multiple_of(k * HEAD_DIM, HEAD_DIM), HEAD_DIM)], keys)
        cols = slice(c * CHUNK, (c + 1) * CHUNK)
        s = s.reshape(TILES_LOCAL, TILE, CHUNK) + bias_v[k, :, :, cols]
        score_v[:, cols] = s.reshape(ROWS, CHUNK)


def score_tiles(k, tiles, first_tile, q_ref, k_ref, slots, bias_s, score_v, p_v, p_s, ell):
    row = lax.broadcasted_iota(jnp.int32, (TILE, CHUNK), 0)
    col = lax.broadcasted_iota(jnp.int32, (TILE, CHUNK), 1)
    diagonal = jnp.where((col < TILE) & (col > row), NEG, 0.0)
    for t in tiles:
        rows = pl.ds(pl.multiple_of(t * TILE, TILE), TILE)
        q = q_ref[rows, pl.ds(pl.multiple_of(k * HEAD_DIM, HEAD_DIM), HEAD_DIM)]
        parts = []
        for c in range(NCHUNK):
            places = [jnp.maximum(first_tile + t - slots[k, 3, c * CHUNK_TILES + n], 0) for n in range(CHUNK_TILES)]
            s = dot_t(q, tiles_of(k_ref, places))
            s = s + bias_s[k, t, :, c * CHUNK:(c + 1) * CHUNK]
            if c == 0:
                s = s + diagonal
            parts.append(s)
        for c in range(NCHUNK):
            parts.append(score_v[rows, c * CHUNK:(c + 1) * CHUNK])
        peak = functools.reduce(jnp.maximum, parts)
        peak = jnp.max(peak, axis=1, keepdims=True)
        total = jnp.zeros((TILE, CHUNK), jnp.float32)
        for c, s in enumerate(parts):
            p = jnp.exp2((s - peak) * EXP_SCALE)
            total += p
            out = p_s if c < NCHUNK else p_v
            cc = c % NCHUNK
            out[k, rows, cc * CHUNK:(cc + 1) * CHUNK] = p.astype(jnp.bfloat16)
        ell[k, rows, :] = jnp.broadcast_to(jnp.sum(total, axis=1, keepdims=True), (TILE, HEAD_DIM))


def value_head(k, first_tile, z, v_ref, slots, p_v, p_s, ell, acc, out_buf, send):
    places = [slots[k, 2, n] for n in range(NVERT)]
    values = tiles_of(v_ref, [jnp.minimum(p, first_tile + TILES_LOCAL - 1) for p in places])
    acc[...] = jnp.dot(p_v[k], values, preferred_element_type=jnp.float32)

    @pl.loop(0, TILES_LOCAL // BATCH)
    def _(batch):
        for m in range(BATCH):
            t = (z + 1 + batch * BATCH + m) % TILES_LOCAL
            rows = pl.ds(pl.multiple_of(t * TILE, TILE), TILE)
            places = [jnp.maximum(first_tile + t - slots[k, 3, n], 0) for n in range(NVERT)]
            o = jnp.dot(p_s[k, rows, :], tiles_of(v_ref, places), preferred_element_type=jnp.float32)
            out_buf[k, rows, :] = ((o + acc[rows, :]) / ell[k, rows, :]).astype(jnp.bfloat16)
        for m in range(BATCH):
            step = batch * BATCH + m + 1

            @pl.when(step < TILES_LOCAL)
            def _():
                send(k, step)


class Gather:
    def __init__(self, me, z, buf, rows, send, recv):
        self.me, self.z, self.buf, self.rows, self.send, self.recv = me, z, buf, rows, send, recv
        self.core = me % 2
        x, y = me // 8, (me // 2) % 4
        c = self.core
        self.a = x * (1 - c) + y * c
        self.b = y * (1 - c) + x * c
        self.started = []

    def at(self, da, db):
        c = self.core
        a, b = (self.a + da) % 4, (self.b + db) % 4
        x = a * (1 - c) + b * c
        y = b * (1 - c) + a * c
        return (x * 4 + y) * 2 + c

    def sibling(self, shard):
        return shard + 1 - 2 * self.core

    def region(self, shard, half):
        if half is None:
            return self.buf.at[shard]
        if half == 0:
            return self.buf.at[shard, pl.ds(0, HALF)]
        return self.buf.at[shard, pl.ds(HALF, self.rows - HALF)]

    def copy(self, shard, half, target, n):
        region = self.region(shard, half)
        return pltpu.make_async_remote_copy(
            src_ref=region, dst_ref=region, send_sem=self.send.at[n],
            recv_sem=self.recv.at[shard, 0 if half is None else half],
            device_id=(target, self.z), device_id_type=MESH)

    def need(self, device, shard):
        return shard // 2 <= device // 2

    def put(self, shard, half, target, cond):
        n = len(self.started)

        @pl.when(cond())
        def _():
            self.copy(shard, half, target, n).start()

        self.started.append((half, cond))

    def got(self, shard, half, cond):
        @pl.when(cond())
        def _():
            self.copy(shard, half, self.sibling(self.me), 0).wait_recv()

    def last_of_ring(self, da):
        return self.at(da, 3 - self.b)

    def passes(self, da, db, half):
        return da != 2 and (half, db) in ((0, 1), (1, -1))

    def put_a(self, half, da):
        self.put(self.me, half, self.at(da, 0), lambda: self.need(self.last_of_ring(da), self.me))

    def put_b(self, da, half, db):
        def cond():
            shard = self.at(da, 0)
            if self.passes(da, db, half):
                return self.need(self.at(0, db), shard) | self.need(self.at(0, 2), shard)
            return self.need(self.at(0, db), shard)

        self.put(self.at(da, 0), half, self.at(0, db), cond)

    def across(self, da, db):
        self.put(self.at(da, db), None, self.sibling(self.me), lambda: self.need(self.me, self.at(da, db)))

    def own(self):
        for half in (0, 1):
            for way in (1, -1):
                self.put_a(half, way)
            for way in (1, -1):
                self.put_b(0, half, way)
        for half in (0, 1):
            self.put_a(half, 2)
        self.across(0, 0)

    def near(self, *das):
        for half in (0, 1):
            for da in das:
                self.got(self.at(da, 0), half, lambda: self.need(self.last_of_ring(0), self.at(da, 0)))
                for way in (1, -1):
                    self.put_b(da, half, way)
        for da in das:
            if da == 2:
                for half in (0, 1):
                    self.put_b(da, half, 2)
            self.across(da, 0)

    def from_b(self, da, db, half):
        shard, beyond = self.at(da, db), self.at(0, -db)
        passes = self.passes(da, -db, half)

        def cond():
            if passes:
                return self.need(self.me, shard) | self.need(beyond, shard)
            return self.need(self.me, shard)

        self.got(shard, half, cond)
        if passes:
            self.put(shard, half, beyond, lambda: self.need(self.at(0, -db), self.at(da, db)))

    def pass_on(self, da):
        self.from_b(da, -1, 0)
        self.from_b(da, 1, 0)
        self.from_b(da, 1, 1)
        self.from_b(da, -1, 1)
        self.across(da, -1)
        self.across(da, 1)

    def far(self, da):
        for half in (0, 1):
            self.got(self.at(da, 2), half, lambda: self.need(self.me, self.at(da, 2)))
        self.across(da, 2)

    def sends(self):
        self.near(-1, 1)
        self.pass_on(0)
        self.near(2)
        self.pass_on(-1)
        self.pass_on(1)

    def ends(self):
        self.far(0)
        self.pass_on(2)
        self.far(-1)
        self.far(1)
        self.far(2)

    def last(self):
        for da in range(4):
            for db in range(4):
                shard = self.sibling(self.at(da, db))
                self.got(shard, None, lambda: self.need(self.me, shard))

    def drain(self):
        for n, (half, cond) in enumerate(self.started):
            @pl.when(cond())
            def _():
                self.copy(self.me, half, self.sibling(self.me), n).wait_send()


N_SENDS = 49
N_SEQ = 32


def fused_kernel(q_hbm, kv_hbm, verts_ref, slashes_ref, codes_ref, out_ref,
                 k_buf, v_buf, q_ref, parts, plan, slots, bias_v, bias_s, score_v, p_v, p_s, ell, acc, out_buf,
                 local_sem, part_send, part_recv, plan_send, plan_recv, k_send, k_recv, v_send, v_recv, out_send, out_recv):
    me = lax.axis_index("seq")
    z = lax.axis_index("help")
    keys = Gather(me, z, k_buf, ROWS, k_send, k_recv)
    values = Gather(me, z, v_buf, ROWS, v_send, v_recv)
    first_tile = me * TILES_LOCAL
    owner = me // GROUP_HEADS

    barrier = pltpu.get_barrier_semaphore()
    peers = [(keys.at(n, 0), z) for n in (1, 2, 3)] + [(keys.at(0, n), z) for n in (1, 2, 3)] + [(keys.sibling(me), z)]
    peers += [(me, (z + n) % 8) for n in range(1, 8)]
    for peer in peers:
        pl.semaphore_signal(barrier, inc=1, device_id=peer, device_id_type=MESH)
    for k in range(GROUP_HEADS):
        @pl.when(me != z * GROUP_HEADS + k)
        def _():
            pl.semaphore_signal(barrier, inc=1, device_id=(z * GROUP_HEADS + k, z), device_id_type=MESH)

    k_cols = pl.ds(pl.multiple_of(z * HEAD_DIM, HEAD_DIM), HEAD_DIM)
    v_cols = pl.ds(pl.multiple_of(z * HEAD_DIM + KV_HEADS * HEAD_DIM, HEAD_DIM), HEAD_DIM)
    q_cols = pl.ds(pl.multiple_of(z * GROUP_HEADS * HEAD_DIM, GROUP_HEADS * HEAD_DIM), GROUP_HEADS * HEAD_DIM)
    k_local = pltpu.make_async_copy(kv_hbm.at[:, k_cols], k_buf.at[me, pl.ds(0, ROWS)], local_sem.at[0])
    v_local = pltpu.make_async_copy(kv_hbm.at[:, v_cols], v_buf.at[me], local_sem.at[1])
    q_local = pltpu.make_async_copy(q_hbm.at[:, q_cols], q_ref, local_sem.at[2])
    k_local.start()
    v_local.start()
    q_local.start()

    width = codes_ref.shape[1]
    tile = lax.broadcasted_iota(jnp.int32, (128, width), 0)
    eye = lax.broadcasted_iota(jnp.int32, (128, 128), 0) == lax.broadcasted_iota(jnp.int32, (128, 128), 1)
    named = []
    for n in range(2):
        group = jnp.broadcast_to(codes_ref[...], (128, width)) - (tile + n * 128) * NGROUP
        bits = jnp.where((group >= 0) & (group < NGROUP), lax.shift_left(1, jnp.clip(group, 0, NGROUP - 1)), 0)
        column = jnp.sum(bits, axis=1, keepdims=True)
        named.append(jnp.sum(jnp.where(eye, jnp.broadcast_to(column, (128, 128)), 0), axis=0, keepdims=True))
    parts[z] = jnp.concatenate(named + [jnp.zeros((6, 128), jnp.int32)], axis=0)

    @pl.when(z != owner)
    def _():
        pl.semaphore_wait(barrier, len(peers))

    @pl.when(z == owner)
    def _():
        pl.semaphore_wait(barrier, len(peers) + N_SEQ - 1)

    part = pltpu.make_async_remote_copy(
        src_ref=parts.at[z], dst_ref=parts.at[z], send_sem=part_send, recv_sem=part_recv.at[z],
        device_id=(me, owner), device_id_type=MESH)

    @pl.when(z != owner)
    def _():
        part.start()

    k_local.wait()
    keys.own()
    mine = me % GROUP_HEADS

    def plan_copy(k, n):
        return pltpu.make_async_remote_copy(
            src_ref=plan.at[k], dst_ref=plan.at[k], send_sem=plan_send.at[n], recv_sem=plan_recv.at[k],
            device_id=((me + n) % N_SEQ, z), device_id_type=MESH)

    @pl.when(z != owner)
    def _():
        part.wait_send()

    @pl.when(z == owner)
    def _():
        for n in range(1, 8):
            other = (z + n) % 8
            pltpu.make_async_remote_copy(
                src_ref=parts.at[other], dst_ref=parts.at[other], send_sem=part_send, recv_sem=part_recv.at[other],
                device_id=(me, other), device_id_type=MESH).wait_recv()
        total = parts[0]
        for n in range(1, 8):
            total += parts[n]
        plan[mine] = total
        plan[mine, 2:3, 0:NVERT] = verts_ref[...]
        plan[mine, 3:4, 0:NVERT] = slashes_ref[...]
        for n in range(1, N_SEQ):
            plan_copy(mine, n).start()

    keys.sends()
    v_local.wait()
    values.own()
    for k in range(GROUP_HEADS):
        @pl.when(me != z * GROUP_HEADS + k)
        def _():
            plan_copy(k, 1).wait_recv()
    slots_copy = pltpu.make_async_copy(plan, slots, local_sem.at[3])
    slots_copy.start()
    make_bias(first_tile, plan, bias_v, bias_s)
    keys.ends()
    slots_copy.wait()
    q_local.wait()
    keys.last()

    def gap(n):
        if n == 0:
            values.near(-1, 1)
        elif n == 1:
            values.pass_on(0)
            values.near(2)
        elif n == 3:
            values.pass_on(-1)
            values.pass_on(1)
        elif n == 4:
            keys.drain()
        elif n == 5:
            values.ends()
            values.last()

    def out_copy(k, n):
        other = (z + n) % 8
        return pltpu.make_async_remote_copy(
            src_ref=out_buf.at[k, pl.ds(pl.multiple_of(other * TILE, TILE), TILE)],
            dst_ref=out_ref.at[:, pl.ds(pl.multiple_of((z * GROUP_HEADS + k) * HEAD_DIM, HEAD_DIM), HEAD_DIM)],
            send_sem=out_send.at[k, n], recv_sem=out_recv.at[z, k], device_id=(me, other), device_id_type=MESH)

    @pl.loop(0, 2 * GROUP_HEADS)
    def _(step):
        @pl.when((step < 3) | (step == 6))
        def _():
            k = step - 3 * (step // 6)
            score_vertical(k, first_tile, q_ref, k_buf, slots, bias_v, score_v)

            @pl.loop(0, TILES_LOCAL // BATCH)
            def _(batch):
                tiles = [batch * BATCH + n for n in range(BATCH)]
                score_tiles(k, tiles, first_tile, q_ref, k_buf, slots, bias_s, score_v, p_v, p_s, ell)
                for n in (0, 1, 3, 4, 5):
                    @pl.when(k * (TILES_LOCAL // BATCH) + batch == n)
                    def _():
                        gap(n)

        @pl.when(((step > 2) & (step < 6)) | (step == 7))
        def _():
            k = step - 3 - step // 7
            value_head(k, first_tile, z, v_buf, slots, p_v, p_s, ell, acc, out_buf, lambda k, n: out_copy(k, n).start())
            cols = pl.ds(pl.multiple_of((z * GROUP_HEADS + k) * HEAD_DIM, HEAD_DIM), HEAD_DIM)
            out_ref[:, cols] = out_buf[k, pl.ds(pl.multiple_of(z * TILE, TILE), TILE), :]

    values.drain()

    @pl.when(z == owner)
    def _():
        for n in range(1, N_SEQ):
            plan_copy(mine, n).wait_send()

    @pl.loop(0, GROUP_HEADS)
    def _(k):
        for n in range(1, 8):
            other = (z + n) % 8
            cols = pl.ds(pl.multiple_of((other * GROUP_HEADS + k) * HEAD_DIM, HEAD_DIM), HEAD_DIM)
            pltpu.make_async_remote_copy(
                src_ref=out_buf.at[k, pl.ds(0, TILE)], dst_ref=out_ref.at[:, cols],
                send_sem=out_send.at[k, n], recv_sem=out_recv.at[other, k], device_id=(me, other),
                device_id_type=MESH).wait_recv()
            out_copy(k, n).wait_send()


def per_device(queries, keys_values, verticals, slashes, units):
    vmem = pl.BlockSpec(memory_space=pltpu.VMEM)
    hbm = pl.BlockSpec(memory_space=pl.ANY)
    dma = pltpu.SemaphoreType.DMA
    seq = lax.axis_size("seq")
    return pl.pallas_call(
        fused_kernel,
        out_shape=jax.ShapeDtypeStruct((TILE, HEADS * HEAD_DIM), jnp.bfloat16),
        in_specs=[hbm, hbm, vmem, vmem, vmem],
        out_specs=vmem,
        scratch_shapes=[
            pltpu.VMEM((seq, ROWS, HEAD_DIM), jnp.bfloat16),
            pltpu.VMEM((seq, ROWS, HEAD_DIM), jnp.bfloat16),
            pltpu.VMEM((ROWS, GROUP_HEADS * HEAD_DIM), jnp.bfloat16),
            pltpu.VMEM((8, 8, 128), jnp.int32),
            pltpu.VMEM((GROUP_HEADS, 8, 128), jnp.int32),
            pltpu.SMEM((GROUP_HEADS, 8, 128), jnp.int32),
            pltpu.VMEM((GROUP_HEADS, TILES_LOCAL, 1, KEYS), jnp.float32),
            pltpu.VMEM((GROUP_HEADS, TILES_LOCAL, 1, KEYS), jnp.float32),
            pltpu.VMEM((ROWS, KEYS), jnp.float32),
            pltpu.VMEM((GROUP_HEADS, ROWS, KEYS), jnp.bfloat16),
            pltpu.VMEM((GROUP_HEADS, ROWS, KEYS), jnp.bfloat16),
            pltpu.VMEM((GROUP_HEADS, ROWS, HEAD_DIM), jnp.float32),
            pltpu.VMEM((ROWS, HEAD_DIM), jnp.float32),
            pltpu.VMEM((GROUP_HEADS, ROWS, HEAD_DIM), jnp.bfloat16),
            dma((4,)), dma, dma((8,)), dma((N_SEQ,)), dma((GROUP_HEADS,)),
            dma((N_SENDS,)), dma((seq, 2)), dma((N_SENDS,)), dma((seq, 2)),
            dma((GROUP_HEADS, 8)), dma((8, GROUP_HEADS)),
        ],
        compiler_params=pltpu.CompilerParams(
            vmem_limit_bytes=56 * 1024 * 1024, collective_id=0, has_side_effects=True),
        name="fused_attention",
    )(queries, keys_values, verticals, slashes, units[0])


def solution(mesh):
    in_specs = (
        P("seq", None),
        P("seq", None),
        P("seq", None),
        P("seq", None),
        P("seq", "help", None),
    )
    out_specs = P(("seq", "help"), None)
    return jax.shard_map(
        per_device, mesh=mesh, in_specs=in_specs, out_specs=out_specs, check_vma=False
    )
```

```python
import functools

import jax
import jax.numpy as jnp
from jax import lax
from jax.experimental import pallas as pl
from jax.experimental.pallas import tpu as pltpu
from jax.sharding import PartitionSpec as P

HEADS = 32
KV_HEADS = 8
HEAD_DIM = 128
TILE = 64
NVERT = 24
NGROUP = 6
GROUP_HEADS = 4
TILES_LOCAL = 8
KEYS = NVERT * TILE
CHUNK = 256
CHUNK_TILES = CHUNK // TILE
NCHUNK = KEYS // CHUNK
ROWS = TILES_LOCAL * TILE
NEG = -1e30
HALF = ROWS // 2
BATCH = TILES_LOCAL // 2
MESH = pl.DeviceIdType.MESH
EXP_SCALE = HEAD_DIM ** -0.5 * 1.4426950408889634


def dot_t(a, b):
    return lax.dot_general(a, b, (((1,), (1,)), ((), ())), preferred_element_type=jnp.float32)


def make_bias(first_tile, plan, bias_v, bias_s):
    lane = lax.broadcasted_iota(jnp.int32, (TILES_LOCAL, 128), 1)
    tile = lax.broadcasted_iota(jnp.int32, (TILES_LOCAL, 128), 0) + first_tile
    slot_of = lax.broadcasted_iota(jnp.int32, (128, KEYS), 1) // TILE
    spread = jnp.where(slot_of == lax.broadcasted_iota(jnp.int32, (128, KEYS), 0), 1.0, 0.0).astype(jnp.bfloat16)
    for k in range(GROUP_HEADS):
        named = jnp.zeros((TILES_LOCAL, 128), jnp.int32)
        for n in range(2):
            mask = jnp.broadcast_to(plan[k, n:n + 1, :], (TILES_LOCAL, 128))
            named += jnp.where(lane + n * 128 == tile, mask, 0)
        named = jnp.sum(named, axis=1, keepdims=True)
        vert = jnp.broadcast_to(plan[k, 2:3, :], (TILES_LOCAL, 128))
        slash = jnp.broadcast_to(plan[k, 3:4, :], (TILES_LOCAL, 128))
        covered = jnp.zeros((TILES_LOCAL, 128), jnp.bool_)
        for n in range(NVERT):
            covered |= (tile - vert) == slash[:, n:n + 1]
        unit = lane // 8
        bit_v = lax.shift_right_logical(jnp.broadcast_to(named, unit.shape), jnp.minimum(unit, 2)) & 1
        bit_s = lax.shift_right_logical(jnp.broadcast_to(named, unit.shape), jnp.minimum(unit + 3, 5)) & 1
        real = lane < NVERT
        att_v = real & (vert <= tile) & jnp.logical_not(covered) & (bit_v == 1)
        att_s = real & (slash <= tile) & (bit_s == 1)
        for att, bias in ((att_v, bias_v), (att_s, bias_s)):
            hot = jnp.where(att, 1.0, 0.0).astype(jnp.bfloat16)
            wide = jnp.dot(hot, spread, preferred_element_type=jnp.float32)
            bias[k] = ((wide - 1.0) * (-NEG)).reshape(TILES_LOCAL, 1, KEYS)


def tile_of(ref, place):
    shard = lax.shift_right_logical(place, 3)
    row = (place & (TILES_LOCAL - 1)) * TILE
    return ref[shard, pl.ds(row, TILE), :]


def tiles_of(ref, places):
    return jnp.concatenate([tile_of(ref, p) for p in places], axis=0)


def score_vertical(k, first_tile, q_ref, k_ref, slots, bias_v, score_v):
    for c in range(NCHUNK):
        places = [slots[k, 2, c * CHUNK_TILES + n] for n in range(CHUNK_TILES)]
        keys = tiles_of(k_ref, [jnp.minimum(p, first_tile + TILES_LOCAL - 1) for p in places])
        s = dot_t(q_ref[:, pl.ds(pl.multiple_of(k * HEAD_DIM, HEAD_DIM), HEAD_DIM)], keys)
        cols = slice(c * CHUNK, (c + 1) * CHUNK)
        s = s.reshape(TILES_LOCAL, TILE, CHUNK) + bias_v[k, :, :, cols]
        score_v[:, cols] = s.reshape(ROWS, CHUNK)


def score_tiles(k, tiles, first_tile, q_ref, k_ref, slots, bias_s, score_v, p_v, p_s, ell):
    row = lax.broadcasted_iota(jnp.int32, (TILE, CHUNK), 0)
    col = lax.broadcasted_iota(jnp.int32, (TILE, CHUNK), 1)
    diagonal = jnp.where((col < TILE) & (col > row), NEG, 0.0)
    for t in tiles:
        rows = pl.ds(pl.multiple_of(t * TILE, TILE), TILE)
        q = q_ref[rows, pl.ds(pl.multiple_of(k * HEAD_DIM, HEAD_DIM), HEAD_DIM)]
        parts = []
        for c in range(NCHUNK):
            places = [jnp.maximum(first_tile + t - slots[k, 3, c * CHUNK_TILES + n], 0) for n in range(CHUNK_TILES)]
            s = dot_t(q, tiles_of(k_ref, places))
            s = s + bias_s[k, t, :, c * CHUNK:(c + 1) * CHUNK]
            if c == 0:
                s = s + diagonal
            parts.append(s)
        for c in range(NCHUNK):
            parts.append(score_v[rows, c * CHUNK:(c + 1) * CHUNK])
        peak = functools.reduce(jnp.maximum, parts)
        peak = jnp.max(peak, axis=1, keepdims=True)
        total = jnp.zeros((TILE, CHUNK), jnp.float32)
        for c, s in enumerate(parts):
            p = jnp.exp2((s - peak) * EXP_SCALE)
            total += p
            out = p_s if c < NCHUNK else p_v
            cc = c % NCHUNK
            out[k, rows, cc * CHUNK:(cc + 1) * CHUNK] = p.astype(jnp.bfloat16)
        ell[k, rows, :] = jnp.broadcast_to(jnp.sum(total, axis=1, keepdims=True), (TILE, HEAD_DIM))


def value_head(k, first_tile, z, v_ref, slots, p_v, p_s, ell, acc, out_buf, send):
    places = [slots[k, 2, n] for n in range(NVERT)]
    values = tiles_of(v_ref, [jnp.minimum(p, first_tile + TILES_LOCAL - 1) for p in places])
    acc[...] = jnp.dot(p_v[k], values, preferred_element_type=jnp.float32)

    @pl.loop(0, TILES_LOCAL // BATCH)
    def _(batch):
        for m in range(BATCH):
            t = (z + 1 + batch * BATCH + m) % TILES_LOCAL
            rows = pl.ds(pl.multiple_of(t * TILE, TILE), TILE)
            places = [jnp.maximum(first_tile + t - slots[k, 3, n], 0) for n in range(NVERT)]
            o = jnp.dot(p_s[k, rows, :], tiles_of(v_ref, places), preferred_element_type=jnp.float32)
            out_buf[k, rows, :] = ((o + acc[rows, :]) / ell[k, rows, :]).astype(jnp.bfloat16)
        for m in range(BATCH):
            step = batch * BATCH + m + 1

            @pl.when(step < TILES_LOCAL)
            def _():
                send(k, step)


class Gather:
    def __init__(self, me, z, buf, rows, send, recv):
        self.me, self.z, self.buf, self.rows, self.send, self.recv = me, z, buf, rows, send, recv
        self.core = me % 2
        x, y = me // 8, (me // 2) % 4
        c = self.core
        self.a = x * (1 - c) + y * c
        self.b = y * (1 - c) + x * c
        self.started = []

    def at(self, da, db):
        c = self.core
        a, b = (self.a + da) % 4, (self.b + db) % 4
        x = a * (1 - c) + b * c
        y = b * (1 - c) + a * c
        return (x * 4 + y) * 2 + c

    def sibling(self, shard):
        return shard + 1 - 2 * self.core

    def region(self, shard, half):
        if half is None:
            return self.buf.at[shard]
        if half == 0:
            return self.buf.at[shard, pl.ds(0, HALF)]
        return self.buf.at[shard, pl.ds(HALF, self.rows - HALF)]

    def copy(self, shard, half, target, n):
        region = self.region(shard, half)
        return pltpu.make_async_remote_copy(
            src_ref=region, dst_ref=region, send_sem=self.send.at[n],
            recv_sem=self.recv.at[shard, 0 if half is None else half],
            device_id=(target, self.z), device_id_type=MESH)

    def need(self, device, shard):
        return shard // 2 <= device // 2

    def put(self, shard, half, target, cond):
        n = len(self.started)

        @pl.when(cond())
        def _():
            self.copy(shard, half, target, n).start()

        self.started.append((half, cond))

    def got(self, shard, half, cond):
        @pl.when(cond())
        def _():
            self.copy(shard, half, self.sibling(self.me), 0).wait_recv()

    def last_of_ring(self, da):
        return self.at(da, 3 - self.b)

    def passes(self, da, db, half):
        return da != 2 and (half, db) in ((0, 1), (1, -1))

    def put_a(self, half, da):
        self.put(self.me, half, self.at(da, 0), lambda: self.need(self.last_of_ring(da), self.me))

    def put_b(self, da, half, db):
        def cond():
            shard = self.at(da, 0)
            if self.passes(da, db, half):
                return self.need(self.at(0, db), shard) | self.need(self.at(0, 2), shard)
            return self.need(self.at(0, db), shard)

        self.put(self.at(da, 0), half, self.at(0, db), cond)

    def across(self, da, db):
        self.put(self.at(da, db), None, self.sibling(self.me), lambda: self.need(self.me, self.at(da, db)))

    def own(self):
        for half in (0, 1):
            for way in (1, -1):
                self.put_a(half, way)
            for way in (1, -1):
                self.put_b(0, half, way)
        for half in (0, 1):
            self.put_a(half, 2)
        self.across(0, 0)

    def near(self, *das):
        for half in (0, 1):
            for da in das:
                self.got(self.at(da, 0), half, lambda: self.need(self.last_of_ring(0), self.at(da, 0)))
                for way in (1, -1):
                    self.put_b(da, half, way)
        for da in das:
            if da == 2:
                for half in (0, 1):
                    self.put_b(da, half, 2)
            self.across(da, 0)

    def from_b(self, da, db, half):
        shard, beyond = self.at(da, db), self.at(0, -db)
        passes = self.passes(da, -db, half)

        def cond():
            if passes:
                return self.need(self.me, shard) | self.need(beyond, shard)
            return self.need(self.me, shard)

        self.got(shard, half, cond)
        if passes:
            self.put(shard, half, beyond, lambda: self.need(self.at(0, -db), self.at(da, db)))

    def pass_on(self, da):
        self.from_b(da, -1, 0)
        self.from_b(da, 1, 0)
        self.from_b(da, 1, 1)
        self.from_b(da, -1, 1)
        self.across(da, -1)
        self.across(da, 1)

    def far(self, da):
        for half in (0, 1):
            self.got(self.at(da, 2), half, lambda: self.need(self.me, self.at(da, 2)))
        self.across(da, 2)

    def sends(self):
        self.near(-1, 1)
        self.pass_on(0)
        self.near(2)
        self.pass_on(-1)
        self.pass_on(1)

    def ends(self):
        self.far(0)
        self.pass_on(2)
        self.far(-1)
        self.far(1)
        self.far(2)

    def last(self):
        for da in range(4):
            for db in range(4):
                shard = self.sibling(self.at(da, db))
                self.got(shard, None, lambda: self.need(self.me, shard))

    def drain(self):
        for n, (half, cond) in enumerate(self.started):
            @pl.when(cond())
            def _():
                self.copy(self.me, half, self.sibling(self.me), n).wait_send()


N_SENDS = 49
N_SEQ = 32


def fused_kernel(q_hbm, kv_hbm, verts_ref, slashes_ref, codes_ref, out_ref,
                 k_buf, v_buf, q_ref, parts, plan, slots, bias_v, bias_s, score_v, p_v, p_s, ell, acc, out_buf,
                 local_sem, part_send, part_recv, plan_send, plan_recv, k_send, k_recv, v_send, v_recv, out_send, out_recv):
    me = lax.axis_index("seq")
    z = lax.axis_index("help")
    keys = Gather(me, z, k_buf, ROWS, k_send, k_recv)
    values = Gather(me, z, v_buf, ROWS, v_send, v_recv)
    first_tile = me * TILES_LOCAL
    owner = me // GROUP_HEADS

    barrier = pltpu.get_barrier_semaphore()
    peers = [(keys.at(n, 0), z) for n in (1, 2, 3)] + [(keys.at(0, n), z) for n in (1, 2, 3)] + [(keys.sibling(me), z)]
    peers += [(me, (z + n) % 8) for n in range(1, 8)]
    for peer in peers:
        pl.semaphore_signal(barrier, inc=1, device_id=peer, device_id_type=MESH)
    for k in range(GROUP_HEADS):
        @pl.when(me != z * GROUP_HEADS + k)
        def _():
            pl.semaphore_signal(barrier, inc=1, device_id=(z * GROUP_HEADS + k, z), device_id_type=MESH)

    k_cols = pl.ds(pl.multiple_of(z * HEAD_DIM, HEAD_DIM), HEAD_DIM)
    v_cols = pl.ds(pl.multiple_of(z * HEAD_DIM + KV_HEADS * HEAD_DIM, HEAD_DIM), HEAD_DIM)
    q_cols = pl.ds(pl.multiple_of(z * GROUP_HEADS * HEAD_DIM, GROUP_HEADS * HEAD_DIM), GROUP_HEADS * HEAD_DIM)
    k_local = pltpu.make_async_copy(kv_hbm.at[:, k_cols], k_buf.at[me, pl.ds(0, ROWS)], local_sem.at[0])
    v_local = pltpu.make_async_copy(kv_hbm.at[:, v_cols], v_buf.at[me], local_sem.at[1])
    q_local = pltpu.make_async_copy(q_hbm.at[:, q_cols], q_ref, local_sem.at[2])
    k_local.start()
    v_local.start()
    q_local.start()

    width = codes_ref.shape[1]
    tile = lax.broadcasted_iota(jnp.int32, (128, width), 0)
    eye = lax.broadcasted_iota(jnp.int32, (128, 128), 0) == lax.broadcasted_iota(jnp.int32, (128, 128), 1)
    named = []
    for n in range(2):
        group = jnp.broadcast_to(codes_ref[...], (128, width)) - (tile + n * 128) * NGROUP
        bits = jnp.where((group >= 0) & (group < NGROUP), lax.shift_left(1, jnp.clip(group, 0, NGROUP - 1)), 0)
        column = jnp.sum(bits, axis=1, keepdims=True)
        named.append(jnp.sum(jnp.where(eye, jnp.broadcast_to(column, (128, 128)), 0), axis=0, keepdims=True))
    parts[z] = jnp.concatenate(named + [jnp.zeros((6, 128), jnp.int32)], axis=0)

    @pl.when(z != owner)
    def _():
        pl.semaphore_wait(barrier, len(peers))

    @pl.when(z == owner)
    def _():
        pl.semaphore_wait(barrier, len(peers) + N_SEQ - 1)

    part = pltpu.make_async_remote_copy(
        src_ref=parts.at[z], dst_ref=parts.at[z], send_sem=part_send, recv_sem=part_recv.at[z],
        device_id=(me, owner), device_id_type=MESH)

    @pl.when(z != owner)
    def _():
        part.start()

    k_local.wait()
    keys.own()
    mine = me % GROUP_HEADS

    def plan_copy(k, n):
        return pltpu.make_async_remote_copy(
            src_ref=plan.at[k], dst_ref=plan.at[k], send_sem=plan_send.at[n], recv_sem=plan_recv.at[k],
            device_id=((me + n) % N_SEQ, z), device_id_type=MESH)

    @pl.when(z != owner)
    def _():
        part.wait_send()

    @pl.when(z == owner)
    def _():
        for n in range(1, 8):
            other = (z + n) % 8
            pltpu.make_async_remote_copy(
                src_ref=parts.at[other], dst_ref=parts.at[other], send_sem=part_send, recv_sem=part_recv.at[other],
                device_id=(me, other), device_id_type=MESH).wait_recv()
        total = parts[0]
        for n in range(1, 8):
            total += parts[n]
        plan[mine] = total
        plan[mine, 2:3, 0:NVERT] = verts_ref[...]
        plan[mine, 3:4, 0:NVERT] = slashes_ref[...]
        for n in range(1, N_SEQ):
            plan_copy(mine, n).start()

    keys.sends()
    v_local.wait()
    values.own()
    for k in range(GROUP_HEADS):
        @pl.when(me != z * GROUP_HEADS + k)
        def _():
            plan_copy(k, 1).wait_recv()
    slots_copy = pltpu.make_async_copy(plan, slots, local_sem.at[3])
    slots_copy.start()
    make_bias(first_tile, plan, bias_v, bias_s)
    keys.ends()
    slots_copy.wait()
    q_local.wait()
    values.near(-1, 1)
    keys.last()

    def gap(n):
        if n == 0:
            values.pass_on(0)
            values.near(2)
        elif n == 2:
            values.pass_on(-1)
            values.pass_on(1)
        elif n == 3:
            keys.drain()
        elif n == 5:
            values.ends()
            values.last()

    def out_copy(k, n):
        other = (z + n) % 8
        return pltpu.make_async_remote_copy(
            src_ref=out_buf.at[k, pl.ds(pl.multiple_of(other * TILE, TILE), TILE)],
            dst_ref=out_ref.at[:, pl.ds(pl.multiple_of((z * GROUP_HEADS + k) * HEAD_DIM, HEAD_DIM), HEAD_DIM)],
            send_sem=out_send.at[k, n], recv_sem=out_recv.at[z, k], device_id=(me, other), device_id_type=MESH)

    @pl.loop(0, 2 * GROUP_HEADS)
    def _(step):
        @pl.when((step < 3) | (step == 6))
        def _():
            k = step - 3 * (step // 6)
            score_vertical(k, first_tile, q_ref, k_buf, slots, bias_v, score_v)

            @pl.loop(0, TILES_LOCAL // BATCH)
            def _(batch):
                tiles = [batch * BATCH + n for n in range(BATCH)]
                score_tiles(k, tiles, first_tile, q_ref, k_buf, slots, bias_s, score_v, p_v, p_s, ell)
                for n in (0, 2, 3, 5):
                    @pl.when(k * (TILES_LOCAL // BATCH) + batch == n)
                    def _():
                        gap(n)

        @pl.when(((step > 2) & (step < 6)) | (step == 7))
        def _():
            k = step - 3 - step // 7
            value_head(k, first_tile, z, v_buf, slots, p_v, p_s, ell, acc, out_buf, lambda k, n: out_copy(k, n).start())
            cols = pl.ds(pl.multiple_of((z * GROUP_HEADS + k) * HEAD_DIM, HEAD_DIM), HEAD_DIM)
            out_ref[:, cols] = out_buf[k, pl.ds(pl.multiple_of(z * TILE, TILE), TILE), :]

    values.drain()

    @pl.when(z == owner)
    def _():
        for n in range(1, N_SEQ):
            plan_copy(mine, n).wait_send()

    @pl.loop(0, GROUP_HEADS)
    def _(k):
        for n in range(1, 8):
            other = (z + n) % 8
            cols = pl.ds(pl.multiple_of((other * GROUP_HEADS + k) * HEAD_DIM, HEAD_DIM), HEAD_DIM)
            pltpu.make_async_remote_copy(
                src_ref=out_buf.at[k, pl.ds(0, TILE)], dst_ref=out_ref.at[:, cols],
                send_sem=out_send.at[k, n], recv_sem=out_recv.at[other, k], device_id=(me, other),
                device_id_type=MESH).wait_recv()
            out_copy(k, n).wait_send()


def per_device(queries, keys_values, verticals, slashes, units):
    vmem = pl.BlockSpec(memory_space=pltpu.VMEM)
    hbm = pl.BlockSpec(memory_space=pl.ANY)
    dma = pltpu.SemaphoreType.DMA
    seq = lax.axis_size("seq")
    return pl.pallas_call(
        fused_kernel,
        out_shape=jax.ShapeDtypeStruct((TILE, HEADS * HEAD_DIM), jnp.bfloat16),
        in_specs=[hbm, hbm, vmem, vmem, vmem],
        out_specs=vmem,
        scratch_shapes=[
            pltpu.VMEM((seq, ROWS, HEAD_DIM), jnp.bfloat16),
            pltpu.VMEM((seq, ROWS, HEAD_DIM), jnp.bfloat16),
            pltpu.VMEM((ROWS, GROUP_HEADS * HEAD_DIM), jnp.bfloat16),
            pltpu.VMEM((8, 8, 128), jnp.int32),
            pltpu.VMEM((GROUP_HEADS, 8, 128), jnp.int32),
            pltpu.SMEM((GROUP_HEADS, 8, 128), jnp.int32),
            pltpu.VMEM((GROUP_HEADS, TILES_LOCAL, 1, KEYS), jnp.float32),
            pltpu.VMEM((GROUP_HEADS, TILES_LOCAL, 1, KEYS), jnp.float32),
            pltpu.VMEM((ROWS, KEYS), jnp.float32),
            pltpu.VMEM((GROUP_HEADS, ROWS, KEYS), jnp.bfloat16),
            pltpu.VMEM((GROUP_HEADS, ROWS, KEYS), jnp.bfloat16),
            pltpu.VMEM((GROUP_HEADS, ROWS, HEAD_DIM), jnp.float32),
            pltpu.VMEM((ROWS, HEAD_DIM), jnp.float32),
            pltpu.VMEM((GROUP_HEADS, ROWS, HEAD_DIM), jnp.bfloat16),
            dma((4,)), dma, dma((8,)), dma((N_SEQ,)), dma((GROUP_HEADS,)),
            dma((N_SENDS,)), dma((seq, 2)), dma((N_SENDS,)), dma((seq, 2)),
            dma((GROUP_HEADS, 8)), dma((8, GROUP_HEADS)),
        ],
        compiler_params=pltpu.CompilerParams(
            vmem_limit_bytes=56 * 1024 * 1024, collective_id=0, has_side_effects=True),
        name="fused_attention",
    )(queries, keys_values, verticals, slashes, units[0])


def solution(mesh):
    in_specs = (
        P("seq", None),
        P("seq", None),
        P("seq", None),
        P("seq", None),
        P("seq", "help", None),
    )
    out_specs = P(("seq", "help"), None)
    return jax.shard_map(
        per_device, mesh=mesh, in_specs=in_specs, out_specs=out_specs, check_vma=False
    )
```

```python
import functools

import jax
import jax.numpy as jnp
from jax import lax
from jax.experimental import pallas as pl
from jax.experimental.pallas import tpu as pltpu
from jax.sharding import PartitionSpec as P

HEADS = 32
KV_HEADS = 8
HEAD_DIM = 128
TILE = 64
NVERT = 24
NGROUP = 6
GROUP_HEADS = 4
TILES_LOCAL = 8
KEYS = NVERT * TILE
CHUNK = 256
CHUNK_TILES = CHUNK // TILE
NCHUNK = KEYS // CHUNK
ROWS = TILES_LOCAL * TILE
NEG = -1e30
HALF = ROWS // 2
BATCH = TILES_LOCAL // 2
MESH = pl.DeviceIdType.MESH
EXP_SCALE = HEAD_DIM ** -0.5 * 1.4426950408889634


def dot_t(a, b):
    return lax.dot_general(a, b, (((1,), (1,)), ((), ())), preferred_element_type=jnp.float32)


def make_bias(first_tile, plan, bias_v, bias_s):
    lane = lax.broadcasted_iota(jnp.int32, (TILES_LOCAL, 128), 1)
    tile = lax.broadcasted_iota(jnp.int32, (TILES_LOCAL, 128), 0) + first_tile
    slot_of = lax.broadcasted_iota(jnp.int32, (128, KEYS), 1) // TILE
    spread = jnp.where(slot_of == lax.broadcasted_iota(jnp.int32, (128, KEYS), 0), 1.0, 0.0).astype(jnp.bfloat16)
    for k in range(GROUP_HEADS):
        named = jnp.zeros((TILES_LOCAL, 128), jnp.int32)
        for n in range(2):
            mask = jnp.broadcast_to(plan[k, n:n + 1, :], (TILES_LOCAL, 128))
            named += jnp.where(lane + n * 128 == tile, mask, 0)
        named = jnp.sum(named, axis=1, keepdims=True)
        vert = jnp.broadcast_to(plan[k, 2:3, :], (TILES_LOCAL, 128))
        slash = jnp.broadcast_to(plan[k, 3:4, :], (TILES_LOCAL, 128))
        covered = jnp.zeros((TILES_LOCAL, 128), jnp.bool_)
        for n in range(NVERT):
            covered |= (tile - vert) == slash[:, n:n + 1]
        unit = lane // 8
        bit_v = lax.shift_right_logical(jnp.broadcast_to(named, unit.shape), jnp.minimum(unit, 2)) & 1
        bit_s = lax.shift_right_logical(jnp.broadcast_to(named, unit.shape), jnp.minimum(unit + 3, 5)) & 1
        real = lane < NVERT
        att_v = real & (vert <= tile) & jnp.logical_not(covered) & (bit_v == 1)
        att_s = real & (slash <= tile) & (bit_s == 1)
        for att, bias in ((att_v, bias_v), (att_s, bias_s)):
            hot = jnp.where(att, 1.0, 0.0).astype(jnp.bfloat16)
            wide = jnp.dot(hot, spread, preferred_element_type=jnp.float32)
            bias[k] = ((wide - 1.0) * (-NEG)).reshape(TILES_LOCAL, 1, KEYS)


def tile_of(ref, place):
    shard = lax.shift_right_logical(place, 3)
    row = (place & (TILES_LOCAL - 1)) * TILE
    return ref[shard, pl.ds(row, TILE), :]


def tiles_of(ref, places):
    return jnp.concatenate([tile_of(ref, p) for p in places], axis=0)


def score_vertical(k, first_tile, q_ref, k_ref, slots, bias_v, score_v):
    for c in range(NCHUNK):
        places = [slots[k, 2, c * CHUNK_TILES + n] for n in range(CHUNK_TILES)]
        keys = tiles_of(k_ref, [jnp.minimum(p, first_tile + TILES_LOCAL - 1) for p in places])
        s = dot_t(q_ref[:, pl.ds(pl.multiple_of(k * HEAD_DIM, HEAD_DIM), HEAD_DIM)], keys)
        cols = slice(c * CHUNK, (c + 1) * CHUNK)
        s = s.reshape(TILES_LOCAL, TILE, CHUNK) + bias_v[k, :, :, cols]
        score_v[:, cols] = s.reshape(ROWS, CHUNK)


def score_tiles(k, tiles, first_tile, q_ref, k_ref, slots, bias_s, score_v, p_v, p_s, ell):
    row = lax.broadcasted_iota(jnp.int32, (TILE, CHUNK), 0)
    col = lax.broadcasted_iota(jnp.int32, (TILE, CHUNK), 1)
    diagonal = jnp.where((col < TILE) & (col > row), NEG, 0.0)
    for t in tiles:
        rows = pl.ds(pl.multiple_of(t * TILE, TILE), TILE)
        q = q_ref[rows, pl.ds(pl.multiple_of(k * HEAD_DIM, HEAD_DIM), HEAD_DIM)]
        parts = []
        for c in range(NCHUNK):
            places = [jnp.maximum(first_tile + t - slots[k, 3, c * CHUNK_TILES + n], 0) for n in range(CHUNK_TILES)]
            s = dot_t(q, tiles_of(k_ref, places))
            s = s + bias_s[k, t, :, c * CHUNK:(c + 1) * CHUNK]
            if c == 0:
                s = s + diagonal
            parts.append(s)
        for c in range(NCHUNK):
            parts.append(score_v[rows, c * CHUNK:(c + 1) * CHUNK])
        peak = functools.reduce(jnp.maximum, parts)
        peak = jnp.max(peak, axis=1, keepdims=True)
        total = jnp.zeros((TILE, CHUNK), jnp.float32)
        for c, s in enumerate(parts):
            p = jnp.exp2((s - peak) * EXP_SCALE)
            total += p
            out = p_s if c < NCHUNK else p_v
            cc = c % NCHUNK
            out[k, rows, cc * CHUNK:(cc + 1) * CHUNK] = p.astype(jnp.bfloat16)
        ell[k, rows, :] = jnp.broadcast_to(jnp.sum(total, axis=1, keepdims=True), (TILE, HEAD_DIM))


def value_head(k, first_tile, z, v_ref, slots, p_v, p_s, ell, acc, out_buf, send):
    places = [slots[k, 2, n] for n in range(NVERT)]
    values = tiles_of(v_ref, [jnp.minimum(p, first_tile + TILES_LOCAL - 1) for p in places])

    @pl.loop(0, TILES_LOCAL // BATCH)
    def _(batch):
        first = (z // BATCH + 1 + batch) % (TILES_LOCAL // BATCH) * BATCH
        half = pl.ds(pl.multiple_of(first * TILE, BATCH * TILE), BATCH * TILE)
        acc[half, :] = jnp.dot(p_v[k, half, :], values, preferred_element_type=jnp.float32)
        for m in range(BATCH):
            t = first + m
            rows = pl.ds(pl.multiple_of(t * TILE, TILE), TILE)
            places = [jnp.maximum(first_tile + t - slots[k, 3, n], 0) for n in range(NVERT)]
            o = jnp.dot(p_s[k, rows, :], tiles_of(v_ref, places), preferred_element_type=jnp.float32)
            out_buf[k, rows, :] = ((o + acc[rows, :]) / ell[k, rows, :]).astype(jnp.bfloat16)
        for m in range(BATCH):
            t = first + m

            @pl.when(t != z)
            def _():
                send(k, (t - z + TILES_LOCAL) % TILES_LOCAL)


class Gather:
    def __init__(self, me, z, buf, rows, send, recv):
        self.me, self.z, self.buf, self.rows, self.send, self.recv = me, z, buf, rows, send, recv
        self.core = me % 2
        x, y = me // 8, (me // 2) % 4
        c = self.core
        self.a = x * (1 - c) + y * c
        self.b = y * (1 - c) + x * c
        self.started = []

    def at(self, da, db):
        c = self.core
        a, b = (self.a + da) % 4, (self.b + db) % 4
        x = a * (1 - c) + b * c
        y = b * (1 - c) + a * c
        return (x * 4 + y) * 2 + c

    def sibling(self, shard):
        return shard + 1 - 2 * self.core

    def region(self, shard, half):
        if half is None:
            return self.buf.at[shard]
        if half == 0:
            return self.buf.at[shard, pl.ds(0, HALF)]
        return self.buf.at[shard, pl.ds(HALF, self.rows - HALF)]

    def copy(self, shard, half, target, n):
        region = self.region(shard, half)
        return pltpu.make_async_remote_copy(
            src_ref=region, dst_ref=region, send_sem=self.send.at[n],
            recv_sem=self.recv.at[shard, 0 if half is None else half],
            device_id=(target, self.z), device_id_type=MESH)

    def need(self, device, shard):
        return shard // 2 <= device // 2

    def put(self, shard, half, target, cond):
        n = len(self.started)

        @pl.when(cond())
        def _():
            self.copy(shard, half, target, n).start()

        self.started.append((half, cond))

    def got(self, shard, half, cond):
        @pl.when(cond())
        def _():
            self.copy(shard, half, self.sibling(self.me), 0).wait_recv()

    def last_of_ring(self, da):
        return self.at(da, 3 - self.b)

    def passes(self, da, db, half):
        return da != 2 and (half, db) in ((0, 1), (1, -1))

    def put_a(self, half, da):
        self.put(self.me, half, self.at(da, 0), lambda: self.need(self.last_of_ring(da), self.me))

    def put_b(self, da, half, db):
        def cond():
            shard = self.at(da, 0)
            if self.passes(da, db, half):
                return self.need(self.at(0, db), shard) | self.need(self.at(0, 2), shard)
            return self.need(self.at(0, db), shard)

        self.put(self.at(da, 0), half, self.at(0, db), cond)

    def across(self, da, db):
        self.put(self.at(da, db), None, self.sibling(self.me), lambda: self.need(self.me, self.at(da, db)))

    def own(self):
        for half in (0, 1):
            for way in (1, -1):
                self.put_a(half, way)
            for way in (1, -1):
                self.put_b(0, half, way)
        for half in (0, 1):
            self.put_a(half, 2)
        self.across(0, 0)

    def near(self, *das):
        for half in (0, 1):
            for da in das:
                self.got(self.at(da, 0), half, lambda: self.need(self.last_of_ring(0), self.at(da, 0)))
                for way in (2, 1, -1) if da == 2 else (1, -1):
                    self.put_b(da, half, way)
        for da in das:
            self.across(da, 0)

    def from_b(self, da, db, half):
        shard, beyond = self.at(da, db), self.at(0, -db)
        passes = self.passes(da, -db, half)

        def cond():
            if passes:
                return self.need(self.me, shard) | self.need(beyond, shard)
            return self.need(self.me, shard)

        self.got(shard, half, cond)
        if passes:
            self.put(shard, half, beyond, lambda: self.need(self.at(0, -db), self.at(da, db)))

    def pass_on(self, da):
        self.from_b(da, -1, 0)
        self.from_b(da, 1, 0)
        self.from_b(da, 1, 1)
        self.from_b(da, -1, 1)
        self.across(da, -1)
        self.across(da, 1)

    def far(self, da):
        for half in (0, 1):
            self.got(self.at(da, 2), half, lambda: self.need(self.me, self.at(da, 2)))
        self.across(da, 2)

    def sends(self):
        self.near(-1, 1)
        self.pass_on(0)
        self.near(2)
        self.pass_on(-1)
        self.pass_on(1)

    def ends(self):
        self.far(0)
        self.pass_on(2)
        self.far(-1)
        self.far(1)
        self.far(2)

    def last(self):
        for da in range(4):
            for db in range(4):
                shard = self.sibling(self.at(da, db))
                self.got(shard, None, lambda: self.need(self.me, shard))

    def drain(self):
        for n, (half, cond) in enumerate(self.started):
            @pl.when(cond())
            def _():
                self.copy(self.me, half, self.sibling(self.me), n).wait_send()


N_SENDS = 49
N_SEQ = 32


def fused_kernel(q_hbm, kv_hbm, verts_ref, slashes_ref, codes_ref, out_ref,
                 k_buf, v_buf, q_ref, parts, plan, slots, bias_v, bias_s, score_v, p_v, p_s, ell, acc, out_buf,
                 local_sem, part_send, part_recv, plan_send, plan_recv, k_send, k_recv, v_send, v_recv, out_send, out_recv):
    me = lax.axis_index("seq")
    z = lax.axis_index("help")
    keys = Gather(me, z, k_buf, ROWS, k_send, k_recv)
    values = Gather(me, z, v_buf, ROWS, v_send, v_recv)
    first_tile = me * TILES_LOCAL
    owner = me // GROUP_HEADS

    barrier = pltpu.get_barrier_semaphore()
    peers = [(keys.at(n, 0), z) for n in (1, 2, 3)] + [(keys.at(0, n), z) for n in (1, 2, 3)] + [(keys.sibling(me), z)]
    peers += [(me, (z + n) % 8) for n in range(1, 8)]
    for peer in peers:
        pl.semaphore_signal(barrier, inc=1, device_id=peer, device_id_type=MESH)
    for k in range(GROUP_HEADS):
        @pl.when(me != z * GROUP_HEADS + k)
        def _():
            pl.semaphore_signal(barrier, inc=1, device_id=(z * GROUP_HEADS + k, z), device_id_type=MESH)

    k_cols = pl.ds(pl.multiple_of(z * HEAD_DIM, HEAD_DIM), HEAD_DIM)
    v_cols = pl.ds(pl.multiple_of(z * HEAD_DIM + KV_HEADS * HEAD_DIM, HEAD_DIM), HEAD_DIM)
    q_cols = pl.ds(pl.multiple_of(z * GROUP_HEADS * HEAD_DIM, GROUP_HEADS * HEAD_DIM), GROUP_HEADS * HEAD_DIM)
    k_local = pltpu.make_async_copy(kv_hbm.at[:, k_cols], k_buf.at[me, pl.ds(0, ROWS)], local_sem.at[0])
    v_local = pltpu.make_async_copy(kv_hbm.at[:, v_cols], v_buf.at[me], local_sem.at[1])
    q_local = pltpu.make_async_copy(q_hbm.at[:, q_cols], q_ref, local_sem.at[2])
    k_local.start()
    v_local.start()
    q_local.start()

    width = codes_ref.shape[1]
    tile = lax.broadcasted_iota(jnp.int32, (128, width), 0)
    eye = lax.broadcasted_iota(jnp.int32, (128, 128), 0) == lax.broadcasted_iota(jnp.int32, (128, 128), 1)
    named = []
    for n in range(2):
        group = jnp.broadcast_to(codes_ref[...], (128, width)) - (tile + n * 128) * NGROUP
        bits = jnp.where((group >= 0) & (group < NGROUP), lax.shift_left(1, jnp.clip(group, 0, NGROUP - 1)), 0)
        column = jnp.sum(bits, axis=1, keepdims=True)
        named.append(jnp.sum(jnp.where(eye, jnp.broadcast_to(column, (128, 128)), 0), axis=0, keepdims=True))
    parts[z] = jnp.concatenate(named + [jnp.zeros((6, 128), jnp.int32)], axis=0)

    @pl.when(z != owner)
    def _():
        pl.semaphore_wait(barrier, len(peers))

    @pl.when(z == owner)
    def _():
        pl.semaphore_wait(barrier, len(peers) + N_SEQ - 1)

    part = pltpu.make_async_remote_copy(
        src_ref=parts.at[z], dst_ref=parts.at[z], send_sem=part_send, recv_sem=part_recv.at[z],
        device_id=(me, owner), device_id_type=MESH)

    @pl.when(z != owner)
    def _():
        part.start()

    k_local.wait()
    keys.own()
    mine = me % GROUP_HEADS

    def plan_copy(k, n):
        return pltpu.make_async_remote_copy(
            src_ref=plan.at[k], dst_ref=plan.at[k], send_sem=plan_send.at[n], recv_sem=plan_recv.at[k],
            device_id=((me + n) % N_SEQ, z), device_id_type=MESH)

    @pl.when(z != owner)
    def _():
        part.wait_send()

    @pl.when(z == owner)
    def _():
        for n in range(1, 8):
            other = (z + n) % 8
            pltpu.make_async_remote_copy(
                src_ref=parts.at[other], dst_ref=parts.at[other], send_sem=part_send, recv_sem=part_recv.at[other],
                device_id=(me, other), device_id_type=MESH).wait_recv()
        total = parts[0]
        for n in range(1, 8):
            total += parts[n]
        plan[mine] = total
        plan[mine, 2:3, 0:NVERT] = verts_ref[...]
        plan[mine, 3:4, 0:NVERT] = slashes_ref[...]
        for n in range(1, N_SEQ):
            plan_copy(mine, n).start()

    keys.sends()
    v_local.wait()
    values.own()
    for k in range(GROUP_HEADS):
        @pl.when(me != z * GROUP_HEADS + k)
        def _():
            plan_copy(k, 1).wait_recv()
    slots_copy = pltpu.make_async_copy(plan, slots, local_sem.at[3])
    slots_copy.start()
    make_bias(first_tile, plan, bias_v, bias_s)
    keys.ends()
    slots_copy.wait()
    q_local.wait()
    values.near(-1, 1)
    keys.last()

    def gap(n):
        if n == 0:
            values.pass_on(0)
            values.near(2)
        elif n == 2:
            values.pass_on(-1)
            values.pass_on(1)
        elif n == 3:
            keys.drain()
        elif n == 5:
            values.ends()
            values.last()

    def out_copy(k, n):
        other = (z + n) % 8
        return pltpu.make_async_remote_copy(
            src_ref=out_buf.at[k, pl.ds(pl.multiple_of(other * TILE, TILE), TILE)],
            dst_ref=out_ref.at[:, pl.ds(pl.multiple_of((z * GROUP_HEADS + k) * HEAD_DIM, HEAD_DIM), HEAD_DIM)],
            send_sem=out_send.at[k, n], recv_sem=out_recv.at[z, k], device_id=(me, other), device_id_type=MESH)

    @pl.loop(0, 2 * GROUP_HEADS)
    def _(step):
        @pl.when((step < 3) | (step == 6))
        def _():
            k = step - 3 * (step // 6)
            score_vertical(k, first_tile, q_ref, k_buf, slots, bias_v, score_v)

            @pl.loop(0, TILES_LOCAL // BATCH)
            def _(batch):
                tiles = [batch * BATCH + n for n in range(BATCH)]
                score_tiles(k, tiles, first_tile, q_ref, k_buf, slots, bias_s, score_v, p_v, p_s, ell)
                for n in (0, 2, 3, 5):
                    @pl.when(k * (TILES_LOCAL // BATCH) + batch == n)
                    def _():
                        gap(n)

        @pl.when(((step > 2) & (step < 6)) | (step == 7))
        def _():
            k = step - 3 - step // 7
            value_head(k, first_tile, z, v_buf, slots, p_v, p_s, ell, acc, out_buf, lambda k, n: out_copy(k, n).start())
            cols = pl.ds(pl.multiple_of((z * GROUP_HEADS + k) * HEAD_DIM, HEAD_DIM), HEAD_DIM)
            out_ref[:, cols] = out_buf[k, pl.ds(pl.multiple_of(z * TILE, TILE), TILE), :]

    values.drain()

    @pl.when(z == owner)
    def _():
        for n in range(1, N_SEQ):
            plan_copy(mine, n).wait_send()

    @pl.loop(0, GROUP_HEADS)
    def _(k):
        for n in range(1, 8):
            other = (z + n) % 8
            cols = pl.ds(pl.multiple_of((other * GROUP_HEADS + k) * HEAD_DIM, HEAD_DIM), HEAD_DIM)
            pltpu.make_async_remote_copy(
                src_ref=out_buf.at[k, pl.ds(0, TILE)], dst_ref=out_ref.at[:, cols],
                send_sem=out_send.at[k, n], recv_sem=out_recv.at[other, k], device_id=(me, other),
                device_id_type=MESH).wait_recv()
            out_copy(k, n).wait_send()


def per_device(queries, keys_values, verticals, slashes, units):
    vmem = pl.BlockSpec(memory_space=pltpu.VMEM)
    hbm = pl.BlockSpec(memory_space=pl.ANY)
    dma = pltpu.SemaphoreType.DMA
    seq = lax.axis_size("seq")
    return pl.pallas_call(
        fused_kernel,
        out_shape=jax.ShapeDtypeStruct((TILE, HEADS * HEAD_DIM), jnp.bfloat16),
        in_specs=[hbm, hbm, vmem, vmem, vmem],
        out_specs=vmem,
        scratch_shapes=[
            pltpu.VMEM((seq, ROWS, HEAD_DIM), jnp.bfloat16),
            pltpu.VMEM((seq, ROWS, HEAD_DIM), jnp.bfloat16),
            pltpu.VMEM((ROWS, GROUP_HEADS * HEAD_DIM), jnp.bfloat16),
            pltpu.VMEM((8, 8, 128), jnp.int32),
            pltpu.VMEM((GROUP_HEADS, 8, 128), jnp.int32),
            pltpu.SMEM((GROUP_HEADS, 8, 128), jnp.int32),
            pltpu.VMEM((GROUP_HEADS, TILES_LOCAL, 1, KEYS), jnp.float32),
            pltpu.VMEM((GROUP_HEADS, TILES_LOCAL, 1, KEYS), jnp.float32),
            pltpu.VMEM((ROWS, KEYS), jnp.float32),
            pltpu.VMEM((GROUP_HEADS, ROWS, KEYS), jnp.bfloat16),
            pltpu.VMEM((GROUP_HEADS, ROWS, KEYS), jnp.bfloat16),
            pltpu.VMEM((GROUP_HEADS, ROWS, HEAD_DIM), jnp.float32),
            pltpu.VMEM((ROWS, HEAD_DIM), jnp.float32),
            pltpu.VMEM((GROUP_HEADS, ROWS, HEAD_DIM), jnp.bfloat16),
            dma((4,)), dma, dma((8,)), dma((N_SEQ,)), dma((GROUP_HEADS,)),
            dma((N_SENDS,)), dma((seq, 2)), dma((N_SENDS,)), dma((seq, 2)),
            dma((GROUP_HEADS, 8)), dma((8, GROUP_HEADS)),
        ],
        compiler_params=pltpu.CompilerParams(
            vmem_limit_bytes=56 * 1024 * 1024, collective_id=0, has_side_effects=True),
        name="fused_attention",
    )(queries, keys_values, verticals, slashes, units[0])


def solution(mesh):
    in_specs = (
        P("seq", None),
        P("seq", None),
        P("seq", None),
        P("seq", None),
        P("seq", "help", None),
    )
    out_specs = P(("seq", "help"), None)
    return jax.shard_map(
        per_device, mesh=mesh, in_specs=in_specs, out_specs=out_specs, check_vma=False
    )
```

```python
import functools

import jax
import jax.numpy as jnp
from jax import lax
from jax.experimental import pallas as pl
from jax.experimental.pallas import tpu as pltpu
from jax.sharding import PartitionSpec as P

HEADS = 32
KV_HEADS = 8
HEAD_DIM = 128
TILE = 64
NVERT = 24
NGROUP = 6
GROUP_HEADS = 4
TILES_LOCAL = 8
KEYS = NVERT * TILE
CHUNK = 256
CHUNK_TILES = CHUNK // TILE
NCHUNK = KEYS // CHUNK
ROWS = TILES_LOCAL * TILE
NEG = -1e30
HALF = ROWS // 2
BATCH = TILES_LOCAL // 2
MESH = pl.DeviceIdType.MESH
EXP_SCALE = HEAD_DIM ** -0.5 * 1.4426950408889634


def dot_t(a, b):
    return lax.dot_general(a, b, (((1,), (1,)), ((), ())), preferred_element_type=jnp.float32)


def make_bias(first_tile, plan, bias_v, bias_s):
    lane = lax.broadcasted_iota(jnp.int32, (TILES_LOCAL, 128), 1)
    tile = lax.broadcasted_iota(jnp.int32, (TILES_LOCAL, 128), 0) + first_tile
    slot_of = lax.broadcasted_iota(jnp.int32, (128, KEYS), 1) // TILE
    spread = jnp.where(slot_of == lax.broadcasted_iota(jnp.int32, (128, KEYS), 0), 1.0, 0.0).astype(jnp.bfloat16)
    for k in range(GROUP_HEADS):
        named = jnp.zeros((TILES_LOCAL, 128), jnp.int32)
        for n in range(2):
            mask = jnp.broadcast_to(plan[k, n:n + 1, :], (TILES_LOCAL, 128))
            named += jnp.where(lane + n * 128 == tile, mask, 0)
        named = jnp.sum(named, axis=1, keepdims=True)
        vert = jnp.broadcast_to(plan[k, 2:3, :], (TILES_LOCAL, 128))
        slash = jnp.broadcast_to(plan[k, 3:4, :], (TILES_LOCAL, 128))
        covered = jnp.zeros((TILES_LOCAL, 128), jnp.bool_)
        for n in range(NVERT):
            covered |= (tile - vert) == slash[:, n:n + 1]
        unit = lane // 8
        bit_v = lax.shift_right_logical(jnp.broadcast_to(named, unit.shape), jnp.minimum(unit, 2)) & 1
        bit_s = lax.shift_right_logical(jnp.broadcast_to(named, unit.shape), jnp.minimum(unit + 3, 5)) & 1
        real = lane < NVERT
        att_v = real & (vert <= tile) & jnp.logical_not(covered) & (bit_v == 1)
        att_s = real & (slash <= tile) & (bit_s == 1)
        for att, bias in ((att_v, bias_v), (att_s, bias_s)):
            hot = jnp.where(att, 1.0, 0.0).astype(jnp.bfloat16)
            wide = jnp.dot(hot, spread, preferred_element_type=jnp.float32)
            bias[k] = ((wide - 1.0) * (-NEG)).reshape(TILES_LOCAL, 1, KEYS)


def tile_of(ref, place):
    shard = lax.shift_right_logical(place, 3)
    row = (place & (TILES_LOCAL - 1)) * TILE
    return ref[shard, pl.ds(row, TILE), :]


def tiles_of(ref, places):
    return jnp.concatenate([tile_of(ref, p) for p in places], axis=0)


def score_vertical(k, first_tile, q_ref, k_ref, slots, bias_v, score_v):
    for c in range(NCHUNK):
        places = [slots[k, 2, c * CHUNK_TILES + n] for n in range(CHUNK_TILES)]
        keys = tiles_of(k_ref, [jnp.minimum(p, first_tile + TILES_LOCAL - 1) for p in places])
        s = dot_t(q_ref[:, pl.ds(pl.multiple_of(k * HEAD_DIM, HEAD_DIM), HEAD_DIM)], keys)
        cols = slice(c * CHUNK, (c + 1) * CHUNK)
        s = s.reshape(TILES_LOCAL, TILE, CHUNK) + bias_v[k, :, :, cols]
        score_v[:, cols] = s.reshape(ROWS, CHUNK)


def score_tiles(k, tiles, first_tile, q_ref, k_ref, slots, bias_s, score_v, p_v, p_s, ell):
    row = lax.broadcasted_iota(jnp.int32, (TILE, CHUNK), 0)
    col = lax.broadcasted_iota(jnp.int32, (TILE, CHUNK), 1)
    diagonal = jnp.where((col < TILE) & (col > row), NEG, 0.0)
    for t in tiles:
        rows = pl.ds(pl.multiple_of(t * TILE, TILE), TILE)
        q = q_ref[rows, pl.ds(pl.multiple_of(k * HEAD_DIM, HEAD_DIM), HEAD_DIM)]
        parts = []
        for c in range(NCHUNK):
            places = [jnp.maximum(first_tile + t - slots[k, 3, c * CHUNK_TILES + n], 0) for n in range(CHUNK_TILES)]
            s = dot_t(q, tiles_of(k_ref, places))
            s = s + bias_s[k, t, :, c * CHUNK:(c + 1) * CHUNK]
            if c == 0:
                s = s + diagonal
            parts.append(s)
        for c in range(NCHUNK):
            parts.append(score_v[rows, c * CHUNK:(c + 1) * CHUNK])
        peak = functools.reduce(jnp.maximum, parts)
        peak = jnp.max(peak, axis=1, keepdims=True)
        total = jnp.zeros((TILE, CHUNK), jnp.float32)
        for c, s in enumerate(parts):
            p = jnp.exp2((s - peak) * EXP_SCALE)
            total += p
            out = p_s if c < NCHUNK else p_v
            cc = c % NCHUNK
            out[k, rows, cc * CHUNK:(cc + 1) * CHUNK] = p.astype(jnp.bfloat16)
        ell[k, rows, :] = jnp.broadcast_to(jnp.sum(total, axis=1, keepdims=True), (TILE, HEAD_DIM))


def value_head(k, first_tile, z, v_ref, slots, p_v, p_s, ell, acc, out_buf, send):
    places = [slots[k, 2, n] for n in range(NVERT)]
    values = tiles_of(v_ref, [jnp.minimum(p, first_tile + TILES_LOCAL - 1) for p in places])

    @pl.loop(0, TILES_LOCAL // BATCH)
    def _(batch):
        first = (z // BATCH + 1 + batch) % (TILES_LOCAL // BATCH) * BATCH
        half = pl.ds(pl.multiple_of(first * TILE, BATCH * TILE), BATCH * TILE)
        acc[half, :] = jnp.dot(p_v[k, half, :], values, preferred_element_type=jnp.float32)
        for m in range(BATCH):
            t = first + m
            rows = pl.ds(pl.multiple_of(t * TILE, TILE), TILE)
            places = [jnp.maximum(first_tile + t - slots[k, 3, n], 0) for n in range(NVERT)]
            o = jnp.dot(p_s[k, rows, :], tiles_of(v_ref, places), preferred_element_type=jnp.float32)
            out_buf[k, rows, :] = ((o + acc[rows, :]) / ell[k, rows, :]).astype(jnp.bfloat16)
        for m in range(BATCH):
            t = first + m

            @pl.when(t != z)
            def _():
                send(k, (t - z + TILES_LOCAL) % TILES_LOCAL)


class Gather:
    def __init__(self, me, z, buf, rows, send, recv):
        self.me, self.z, self.buf, self.rows, self.send, self.recv = me, z, buf, rows, send, recv
        self.core = me % 2
        x, y = me // 8, (me // 2) % 4
        c = self.core
        self.a = x * (1 - c) + y * c
        self.b = y * (1 - c) + x * c
        self.started = []

    def at(self, da, db):
        c = self.core
        a, b = (self.a + da) % 4, (self.b + db) % 4
        x = a * (1 - c) + b * c
        y = b * (1 - c) + a * c
        return (x * 4 + y) * 2 + c

    def sibling(self, shard):
        return shard + 1 - 2 * self.core

    def region(self, shard, half):
        if half is None:
            return self.buf.at[shard]
        if half == 0:
            return self.buf.at[shard, pl.ds(0, HALF)]
        return self.buf.at[shard, pl.ds(HALF, self.rows - HALF)]

    def copy(self, shard, half, target, n):
        region = self.region(shard, half)
        return pltpu.make_async_remote_copy(
            src_ref=region, dst_ref=region, send_sem=self.send.at[n],
            recv_sem=self.recv.at[shard, 0 if half is None else half],
            device_id=(target, self.z), device_id_type=MESH)

    def need(self, device, shard):
        return shard // 2 <= device // 2

    def put(self, shard, half, target, cond):
        n = len(self.started)

        @pl.when(cond())
        def _():
            self.copy(shard, half, target, n).start()

        self.started.append((half, cond))

    def got(self, shard, half, cond):
        @pl.when(cond())
        def _():
            self.copy(shard, half, self.sibling(self.me), 0).wait_recv()

    def last_of_ring(self, da):
        return self.at(da, 3 - self.b)

    def passes(self, da, db, half):
        return da != 2 and (half, db) in ((0, 1), (1, -1))

    def put_a(self, half, da):
        self.put(self.me, half, self.at(da, 0), lambda: self.need(self.last_of_ring(da), self.me))

    def put_b(self, da, half, db):
        def cond():
            shard = self.at(da, 0)
            if self.passes(da, db, half):
                return self.need(self.at(0, db), shard) | self.need(self.at(0, 2), shard)
            return self.need(self.at(0, db), shard)

        self.put(self.at(da, 0), half, self.at(0, db), cond)

    def across(self, da, db):
        self.put(self.at(da, db), None, self.sibling(self.me), lambda: self.need(self.me, self.at(da, db)))

    def own(self):
        for half in (0, 1):
            for way in (1, -1):
                self.put_a(half, way)
            for way in (1, -1):
                self.put_b(0, half, way)
        for half in (0, 1):
            self.put_a(half, 2)
        self.across(0, 0)

    def near(self, *das):
        for half in (0, 1):
            for da in das:
                self.got(self.at(da, 0), half, lambda: self.need(self.last_of_ring(0), self.at(da, 0)))
                for way in (2, 1, -1) if da == 2 else (1, -1):
                    self.put_b(da, half, way)
        for da in das:
            self.across(da, 0)

    def from_b(self, da, db, half):
        shard, beyond = self.at(da, db), self.at(0, -db)
        passes = self.passes(da, -db, half)

        def cond():
            if passes:
                return self.need(self.me, shard) | self.need(beyond, shard)
            return self.need(self.me, shard)

        self.got(shard, half, cond)
        if passes:
            self.put(shard, half, beyond, lambda: self.need(self.at(0, -db), self.at(da, db)))

    def pass_on(self, da):
        self.from_b(da, -1, 0)
        self.from_b(da, 1, 0)
        self.from_b(da, 1, 1)
        self.from_b(da, -1, 1)
        self.across(da, -1)
        self.across(da, 1)

    def far(self, da):
        for half in (0, 1):
            self.got(self.at(da, 2), half, lambda: self.need(self.me, self.at(da, 2)))
        self.across(da, 2)

    def sends(self):
        self.near(-1, 1)
        self.pass_on(0)
        self.near(2)
        self.pass_on(-1)
        self.pass_on(1)

    def ends(self):
        self.far(0)
        self.pass_on(2)
        self.far(-1)
        self.far(1)
        self.far(2)

    def last(self):
        for da in range(4):
            for db in range(4):
                shard = self.sibling(self.at(da, db))
                self.got(shard, None, lambda: self.need(self.me, shard))

    def drain(self):
        for n, (half, cond) in enumerate(self.started):
            @pl.when(cond())
            def _():
                self.copy(self.me, half, self.sibling(self.me), n).wait_send()


N_SENDS = 49
N_SEQ = 32


def fused_kernel(q_hbm, kv_hbm, verts_ref, slashes_ref, codes_ref, out_ref,
                 k_buf, v_buf, q_ref, parts, plan, slots, bias_v, bias_s, score_v, p_v, p_s, ell, acc, out_buf,
                 local_sem, part_send, part_recv, plan_send, plan_recv, k_send, k_recv, v_send, v_recv, out_send, out_recv):
    me = lax.axis_index("seq")
    z = lax.axis_index("help")
    keys = Gather(me, z, k_buf, ROWS, k_send, k_recv)
    values = Gather(me, z, v_buf, ROWS, v_send, v_recv)
    first_tile = me * TILES_LOCAL
    owner = me // GROUP_HEADS

    barrier = pltpu.get_barrier_semaphore()
    peers = [(keys.at(n, 0), z) for n in (1, 2, 3)] + [(keys.at(0, n), z) for n in (1, 2, 3)] + [(keys.sibling(me), z)]
    peers += [(me, (z + n) % 8) for n in range(1, 8)]
    for peer in peers:
        pl.semaphore_signal(barrier, inc=1, device_id=peer, device_id_type=MESH)
    for k in range(GROUP_HEADS):
        @pl.when(me != z * GROUP_HEADS + k)
        def _():
            pl.semaphore_signal(barrier, inc=1, device_id=(z * GROUP_HEADS + k, z), device_id_type=MESH)

    k_cols = pl.ds(pl.multiple_of(z * HEAD_DIM, HEAD_DIM), HEAD_DIM)
    v_cols = pl.ds(pl.multiple_of(z * HEAD_DIM + KV_HEADS * HEAD_DIM, HEAD_DIM), HEAD_DIM)
    q_cols = pl.ds(pl.multiple_of(z * GROUP_HEADS * HEAD_DIM, GROUP_HEADS * HEAD_DIM), GROUP_HEADS * HEAD_DIM)
    k_local = pltpu.make_async_copy(kv_hbm.at[:, k_cols], k_buf.at[me, pl.ds(0, ROWS)], local_sem.at[0])
    v_local = pltpu.make_async_copy(kv_hbm.at[:, v_cols], v_buf.at[me], local_sem.at[1])
    q_local = pltpu.make_async_copy(q_hbm.at[:, q_cols], q_ref, local_sem.at[2])
    k_local.start()
    v_local.start()
    q_local.start()

    width = codes_ref.shape[1]
    tile = lax.broadcasted_iota(jnp.int32, (128, width), 0)
    eye = lax.broadcasted_iota(jnp.int32, (128, 128), 0) == lax.broadcasted_iota(jnp.int32, (128, 128), 1)
    named = []
    for n in range(2):
        group = jnp.broadcast_to(codes_ref[...], (128, width)) - (tile + n * 128) * NGROUP
        bits = jnp.where((group >= 0) & (group < NGROUP), lax.shift_left(1, jnp.clip(group, 0, NGROUP - 1)), 0)
        column = jnp.sum(bits, axis=1, keepdims=True)
        named.append(jnp.sum(jnp.where(eye, jnp.broadcast_to(column, (128, 128)), 0), axis=0, keepdims=True))
    parts[z] = jnp.concatenate(named + [jnp.zeros((6, 128), jnp.int32)], axis=0)

    @pl.when(z != owner)
    def _():
        pl.semaphore_wait(barrier, len(peers))

    @pl.when(z == owner)
    def _():
        pl.semaphore_wait(barrier, len(peers) + N_SEQ - 1)

    part = pltpu.make_async_remote_copy(
        src_ref=parts.at[z], dst_ref=parts.at[z], send_sem=part_send, recv_sem=part_recv.at[z],
        device_id=(me, owner), device_id_type=MESH)

    @pl.when(z != owner)
    def _():
        part.start()

    k_local.wait()
    keys.own()
    mine = me % GROUP_HEADS

    def plan_copy(k, n):
        return pltpu.make_async_remote_copy(
            src_ref=plan.at[k], dst_ref=plan.at[k], send_sem=plan_send.at[n], recv_sem=plan_recv.at[k],
            device_id=((me + n) % N_SEQ, z), device_id_type=MESH)

    @pl.when(z != owner)
    def _():
        part.wait_send()

    @pl.when(z == owner)
    def _():
        for n in range(1, 8):
            other = (z + n) % 8
            pltpu.make_async_remote_copy(
                src_ref=parts.at[other], dst_ref=parts.at[other], send_sem=part_send, recv_sem=part_recv.at[other],
                device_id=(me, other), device_id_type=MESH).wait_recv()
        total = parts[0]
        for n in range(1, 8):
            total += parts[n]
        plan[mine] = total
        plan[mine, 2:3, 0:NVERT] = verts_ref[...]
        plan[mine, 3:4, 0:NVERT] = slashes_ref[...]
        for n in range(1, N_SEQ):
            plan_copy(mine, n).start()

    keys.sends()
    v_local.wait()
    values.own()
    for k in range(GROUP_HEADS):
        @pl.when(me != z * GROUP_HEADS + k)
        def _():
            plan_copy(k, 1).wait_recv()
    slots_copy = pltpu.make_async_copy(plan, slots, local_sem.at[3])
    slots_copy.start()
    make_bias(first_tile, plan, bias_v, bias_s)
    keys.ends()
    slots_copy.wait()
    q_local.wait()
    values.near(-1, 1)
    keys.last()

    def gap(n):
        if n == 0:
            values.pass_on(0)
            values.near(2)
        elif n == 2:
            values.pass_on(-1)
            values.pass_on(1)
        elif n == 4:
            values.far(0)
            values.pass_on(2)
        elif n == 5:
            values.far(-1)
            values.far(1)
            values.far(2)
            values.last()

    def out_copy(k, n):
        other = (z + n) % 8
        return pltpu.make_async_remote_copy(
            src_ref=out_buf.at[k, pl.ds(pl.multiple_of(other * TILE, TILE), TILE)],
            dst_ref=out_ref.at[:, pl.ds(pl.multiple_of((z * GROUP_HEADS + k) * HEAD_DIM, HEAD_DIM), HEAD_DIM)],
            send_sem=out_send.at[k, n], recv_sem=out_recv.at[z, k], device_id=(me, other), device_id_type=MESH)

    @pl.loop(0, 2 * GROUP_HEADS)
    def _(step):
        @pl.when((step < 3) | (step == 6))
        def _():
            k = step - 3 * (step // 6)
            score_vertical(k, first_tile, q_ref, k_buf, slots, bias_v, score_v)

            @pl.loop(0, TILES_LOCAL // BATCH)
            def _(batch):
                tiles = [batch * BATCH + n for n in range(BATCH)]
                score_tiles(k, tiles, first_tile, q_ref, k_buf, slots, bias_s, score_v, p_v, p_s, ell)
                for n in (0, 2, 4, 5):
                    @pl.when(k * (TILES_LOCAL // BATCH) + batch == n)
                    def _():
                        gap(n)

        @pl.when(((step > 2) & (step < 6)) | (step == 7))
        def _():
            k = step - 3 - step // 7
            value_head(k, first_tile, z, v_buf, slots, p_v, p_s, ell, acc, out_buf, lambda k, n: out_copy(k, n).start())
            cols = pl.ds(pl.multiple_of((z * GROUP_HEADS + k) * HEAD_DIM, HEAD_DIM), HEAD_DIM)
            out_ref[:, cols] = out_buf[k, pl.ds(pl.multiple_of(z * TILE, TILE), TILE), :]

    keys.drain()
    values.drain()

    @pl.when(z == owner)
    def _():
        for n in range(1, N_SEQ):
            plan_copy(mine, n).wait_send()

    @pl.loop(0, GROUP_HEADS)
    def _(k):
        for n in range(1, 8):
            other = (z + n) % 8
            cols = pl.ds(pl.multiple_of((other * GROUP_HEADS + k) * HEAD_DIM, HEAD_DIM), HEAD_DIM)
            pltpu.make_async_remote_copy(
                src_ref=out_buf.at[k, pl.ds(0, TILE)], dst_ref=out_ref.at[:, cols],
                send_sem=out_send.at[k, n], recv_sem=out_recv.at[other, k], device_id=(me, other),
                device_id_type=MESH).wait_recv()
            out_copy(k, n).wait_send()


def per_device(queries, keys_values, verticals, slashes, units):
    vmem = pl.BlockSpec(memory_space=pltpu.VMEM)
    hbm = pl.BlockSpec(memory_space=pl.ANY)
    dma = pltpu.SemaphoreType.DMA
    seq = lax.axis_size("seq")
    return pl.pallas_call(
        fused_kernel,
        out_shape=jax.ShapeDtypeStruct((TILE, HEADS * HEAD_DIM), jnp.bfloat16),
        in_specs=[hbm, hbm, vmem, vmem, vmem],
        out_specs=vmem,
        scratch_shapes=[
            pltpu.VMEM((seq, ROWS, HEAD_DIM), jnp.bfloat16),
            pltpu.VMEM((seq, ROWS, HEAD_DIM), jnp.bfloat16),
            pltpu.VMEM((ROWS, GROUP_HEADS * HEAD_DIM), jnp.bfloat16),
            pltpu.VMEM((8, 8, 128), jnp.int32),
            pltpu.VMEM((GROUP_HEADS, 8, 128), jnp.int32),
            pltpu.SMEM((GROUP_HEADS, 8, 128), jnp.int32),
            pltpu.VMEM((GROUP_HEADS, TILES_LOCAL, 1, KEYS), jnp.float32),
            pltpu.VMEM((GROUP_HEADS, TILES_LOCAL, 1, KEYS), jnp.float32),
            pltpu.VMEM((ROWS, KEYS), jnp.float32),
            pltpu.VMEM((GROUP_HEADS, ROWS, KEYS), jnp.bfloat16),
            pltpu.VMEM((GROUP_HEADS, ROWS, KEYS), jnp.bfloat16),
            pltpu.VMEM((GROUP_HEADS, ROWS, HEAD_DIM), jnp.float32),
            pltpu.VMEM((ROWS, HEAD_DIM), jnp.float32),
            pltpu.VMEM((GROUP_HEADS, ROWS, HEAD_DIM), jnp.bfloat16),
            dma((4,)), dma, dma((8,)), dma((N_SEQ,)), dma((GROUP_HEADS,)),
            dma((N_SENDS,)), dma((seq, 2)), dma((N_SENDS,)), dma((seq, 2)),
            dma((GROUP_HEADS, 8)), dma((8, GROUP_HEADS)),
        ],
        compiler_params=pltpu.CompilerParams(
            vmem_limit_bytes=56 * 1024 * 1024, collective_id=0, has_side_effects=True),
        name="fused_attention",
    )(queries, keys_values, verticals, slashes, units[0])


def solution(mesh):
    in_specs = (
        P("seq", None),
        P("seq", None),
        P("seq", None),
        P("seq", None),
        P("seq", "help", None),
    )
    out_specs = P(("seq", "help"), None)
    return jax.shard_map(
        per_device, mesh=mesh, in_specs=in_specs, out_specs=out_specs, check_vma=False
    )
```

```python
import functools

import jax
import jax.numpy as jnp
from jax import lax
from jax.experimental import pallas as pl
from jax.experimental.pallas import tpu as pltpu
from jax.sharding import PartitionSpec as P

HEADS = 32
KV_HEADS = 8
HEAD_DIM = 128
TILE = 64
NVERT = 24
NGROUP = 6
GROUP_HEADS = 4
TILES_LOCAL = 8
KEYS = NVERT * TILE
CHUNK = 256
CHUNK_TILES = CHUNK // TILE
NCHUNK = KEYS // CHUNK
ROWS = TILES_LOCAL * TILE
NEG = -1e30
HALF = ROWS // 2
BATCH = TILES_LOCAL // 2
MESH = pl.DeviceIdType.MESH
EXP_SCALE = HEAD_DIM ** -0.5 * 1.4426950408889634


def dot_t(a, b):
    return lax.dot_general(a, b, (((1,), (1,)), ((), ())), preferred_element_type=jnp.float32)


def make_bias(first_tile, plan, bias_v, bias_s):
    lane = lax.broadcasted_iota(jnp.int32, (TILES_LOCAL, 128), 1)
    tile = lax.broadcasted_iota(jnp.int32, (TILES_LOCAL, 128), 0) + first_tile
    slot_of = lax.broadcasted_iota(jnp.int32, (128, KEYS), 1) // TILE
    spread = jnp.where(slot_of == lax.broadcasted_iota(jnp.int32, (128, KEYS), 0), 1.0, 0.0).astype(jnp.bfloat16)
    for k in range(GROUP_HEADS):
        named = jnp.zeros((TILES_LOCAL, 128), jnp.int32)
        for n in range(2):
            mask = jnp.broadcast_to(plan[k, n:n + 1, :], (TILES_LOCAL, 128))
            named += jnp.where(lane + n * 128 == tile, mask, 0)
        named = jnp.sum(named, axis=1, keepdims=True)
        vert = jnp.broadcast_to(plan[k, 2:3, :], (TILES_LOCAL, 128))
        slash = jnp.broadcast_to(plan[k, 3:4, :], (TILES_LOCAL, 128))
        covered = jnp.zeros((TILES_LOCAL, 128), jnp.bool_)
        for n in range(NVERT):
            covered |= (tile - vert) == slash[:, n:n + 1]
        unit = lane // 8
        bit_v = lax.shift_right_logical(jnp.broadcast_to(named, unit.shape), jnp.minimum(unit, 2)) & 1
        bit_s = lax.shift_right_logical(jnp.broadcast_to(named, unit.shape), jnp.minimum(unit + 3, 5)) & 1
        real = lane < NVERT
        att_v = real & (vert <= tile) & jnp.logical_not(covered) & (bit_v == 1)
        att_s = real & (slash <= tile) & (bit_s == 1)
        for att, bias in ((att_v, bias_v), (att_s, bias_s)):
            hot = jnp.where(att, 1.0, 0.0).astype(jnp.bfloat16)
            wide = jnp.dot(hot, spread, preferred_element_type=jnp.float32)
            bias[k] = ((wide - 1.0) * (-NEG)).reshape(TILES_LOCAL, 1, KEYS)


def tile_of(ref, place):
    shard = lax.shift_right_logical(place, 3)
    row = (place & (TILES_LOCAL - 1)) * TILE
    return ref[shard, pl.ds(row, TILE), :]


def tiles_of(ref, places):
    return jnp.concatenate([tile_of(ref, p) for p in places], axis=0)


def score_vertical(k, first_tile, q_ref, k_ref, slots, bias_v, score_v):
    for c in range(NCHUNK):
        places = [slots[k, 2, c * CHUNK_TILES + n] for n in range(CHUNK_TILES)]
        keys = tiles_of(k_ref, [jnp.minimum(p, first_tile + TILES_LOCAL - 1) for p in places])
        s = dot_t(q_ref[:, pl.ds(pl.multiple_of(k * HEAD_DIM, HEAD_DIM), HEAD_DIM)], keys)
        cols = slice(c * CHUNK, (c + 1) * CHUNK)
        s = s.reshape(TILES_LOCAL, TILE, CHUNK) + bias_v[k, :, :, cols]
        score_v[:, cols] = s.reshape(ROWS, CHUNK)


def score_tiles(k, tiles, first_tile, q_ref, k_ref, slots, bias_s, score_v, p_v, p_s, ell):
    row = lax.broadcasted_iota(jnp.int32, (TILE, CHUNK), 0)
    col = lax.broadcasted_iota(jnp.int32, (TILE, CHUNK), 1)
    diagonal = jnp.where((col < TILE) & (col > row), NEG, 0.0)
    for t in tiles:
        rows = pl.ds(pl.multiple_of(t * TILE, TILE), TILE)
        q = q_ref[rows, pl.ds(pl.multiple_of(k * HEAD_DIM, HEAD_DIM), HEAD_DIM)]
        parts = []
        for c in range(NCHUNK):
            places = [jnp.maximum(first_tile + t - slots[k, 3, c * CHUNK_TILES + n], 0) for n in range(CHUNK_TILES)]
            s = dot_t(q, tiles_of(k_ref, places))
            s = s + bias_s[k, t, :, c * CHUNK:(c + 1) * CHUNK]
            if c == 0:
                s = s + diagonal
            parts.append(s)
        for c in range(NCHUNK):
            parts.append(score_v[rows, c * CHUNK:(c + 1) * CHUNK])
        peak = functools.reduce(jnp.maximum, parts)
        peak = jnp.max(peak, axis=1, keepdims=True)
        total = jnp.zeros((TILE, CHUNK), jnp.float32)
        for c, s in enumerate(parts):
            p = jnp.exp2((s - peak) * EXP_SCALE)
            total += p
            out = p_s if c < NCHUNK else p_v
            cc = c % NCHUNK
            out[k, rows, cc * CHUNK:(cc + 1) * CHUNK] = p.astype(jnp.bfloat16)
        ell[k, rows, :] = jnp.broadcast_to(jnp.sum(total, axis=1, keepdims=True), (TILE, HEAD_DIM))


def value_head(k, first_tile, z, v_ref, slots, p_v, p_s, ell, acc, out_buf, send):
    places = [slots[k, 2, n] for n in range(NVERT)]
    values = tiles_of(v_ref, [jnp.minimum(p, first_tile + TILES_LOCAL - 1) for p in places])

    @pl.loop(0, TILES_LOCAL // BATCH)
    def _(batch):
        first = (z // BATCH + 1 + batch) % (TILES_LOCAL // BATCH) * BATCH
        half = pl.ds(pl.multiple_of(first * TILE, BATCH * TILE), BATCH * TILE)
        acc[half, :] = jnp.dot(p_v[k, half, :], values, preferred_element_type=jnp.float32)
        for m in range(BATCH):
            t = first + m
            rows = pl.ds(pl.multiple_of(t * TILE, TILE), TILE)
            places = [jnp.maximum(first_tile + t - slots[k, 3, n], 0) for n in range(NVERT)]
            o = jnp.dot(p_s[k, rows, :], tiles_of(v_ref, places), preferred_element_type=jnp.float32)
            out_buf[k, rows, :] = ((o + acc[rows, :]) / ell[k, rows, :]).astype(jnp.bfloat16)
        for m in range(BATCH):
            t = first + m

            @pl.when(t != z)
            def _():
                send(k, (t - z + TILES_LOCAL) % TILES_LOCAL)


class Gather:
    def __init__(self, me, z, buf, rows, send, recv):
        self.me, self.z, self.buf, self.rows, self.send, self.recv = me, z, buf, rows, send, recv
        self.core = me % 2
        x, y = me // 8, (me // 2) % 4
        c = self.core
        self.a = x * (1 - c) + y * c
        self.b = y * (1 - c) + x * c
        self.started = []

    def at(self, da, db):
        c = self.core
        a, b = (self.a + da) % 4, (self.b + db) % 4
        x = a * (1 - c) + b * c
        y = b * (1 - c) + a * c
        return (x * 4 + y) * 2 + c

    def sibling(self, shard):
        return shard + 1 - 2 * self.core

    def region(self, shard, half):
        if half is None:
            return self.buf.at[shard]
        if half == 0:
            return self.buf.at[shard, pl.ds(0, HALF)]
        return self.buf.at[shard, pl.ds(HALF, self.rows - HALF)]

    def copy(self, shard, half, target, n):
        region = self.region(shard, half)
        return pltpu.make_async_remote_copy(
            src_ref=region, dst_ref=region, send_sem=self.send.at[n],
            recv_sem=self.recv.at[shard, 0 if half is None else half],
            device_id=(target, self.z), device_id_type=MESH)

    def need(self, device, shard):
        return shard // 2 <= device // 2

    def put(self, shard, half, target, cond):
        n = len(self.started)

        @pl.when(cond())
        def _():
            self.copy(shard, half, target, n).start()

        self.started.append((half, cond))

    def got(self, shard, half, cond):
        @pl.when(cond())
        def _():
            self.copy(shard, half, self.sibling(self.me), 0).wait_recv()

    def last_of_ring(self, da):
        return self.at(da, 3 - self.b)

    def passes(self, da, db, half):
        return da != 2 and (half, db) in ((0, 1), (1, -1))

    def put_a(self, half, da):
        self.put(self.me, half, self.at(da, 0), lambda: self.need(self.last_of_ring(da), self.me))

    def put_b(self, da, half, db):
        def cond():
            shard = self.at(da, 0)
            if self.passes(da, db, half):
                return self.need(self.at(0, db), shard) | self.need(self.at(0, 2), shard)
            return self.need(self.at(0, db), shard)

        self.put(self.at(da, 0), half, self.at(0, db), cond)

    def across(self, da, db):
        self.put(self.at(da, db), None, self.sibling(self.me), lambda: self.need(self.me, self.at(da, db)))

    def own(self):
        for half in (0, 1):
            for way in (1, -1):
                self.put_a(half, way)
            for way in (1, -1):
                self.put_b(0, half, way)
        for half in (0, 1):
            self.put_a(half, 2)
        self.across(0, 0)

    def near(self, *das):
        for half in (0, 1):
            for da in das:
                self.got(self.at(da, 0), half, lambda: self.need(self.last_of_ring(0), self.at(da, 0)))
                for way in (2, 1, -1) if da == 2 else (1, -1):
                    self.put_b(da, half, way)
        for da in das:
            self.across(da, 0)

    def from_b(self, da, db, half):
        shard, beyond = self.at(da, db), self.at(0, -db)
        passes = self.passes(da, -db, half)

        def cond():
            if passes:
                return self.need(self.me, shard) | self.need(beyond, shard)
            return self.need(self.me, shard)

        self.got(shard, half, cond)
        if passes:
            self.put(shard, half, beyond, lambda: self.need(self.at(0, -db), self.at(da, db)))

    def pass_on(self, da):
        self.from_b(da, -1, 0)
        self.from_b(da, 1, 0)
        self.from_b(da, 1, 1)
        self.from_b(da, -1, 1)
        self.across(da, -1)
        self.across(da, 1)

    def far(self, da):
        for half in (0, 1):
            shard = self.at(da, 2)
            self.got(shard, half, lambda: self.need(self.me, shard))
            self.put(shard, half, self.sibling(self.me), lambda: self.need(self.me, self.at(da, 2)))

    def sends(self):
        self.near(-1, 1)
        self.pass_on(0)
        self.near(2)
        self.pass_on(-1)
        self.pass_on(1)

    def ends(self):
        self.far(0)
        self.pass_on(2)
        self.far(-1)
        self.far(1)
        self.far(2)

    def last(self):
        for da in range(4):
            for db in range(4):
                shard = self.sibling(self.at(da, db))
                for half in (0, 1) if da == 2 else (None,):
                    self.got(shard, half, lambda: self.need(self.me, shard))

    def drain(self):
        for n, (half, cond) in enumerate(self.started):
            @pl.when(cond())
            def _():
                self.copy(self.me, half, self.sibling(self.me), n).wait_send()


N_SENDS = 53
N_SEQ = 32


def fused_kernel(q_hbm, kv_hbm, verts_ref, slashes_ref, codes_ref, out_ref,
                 k_buf, v_buf, q_ref, parts, plan, slots, bias_v, bias_s, score_v, p_v, p_s, ell, acc, out_buf,
                 local_sem, part_send, part_recv, plan_send, plan_recv, k_send, k_recv, v_send, v_recv, out_send, out_recv):
    me = lax.axis_index("seq")
    z = lax.axis_index("help")
    keys = Gather(me, z, k_buf, ROWS, k_send, k_recv)
    values = Gather(me, z, v_buf, ROWS, v_send, v_recv)
    first_tile = me * TILES_LOCAL
    owner = me // GROUP_HEADS

    barrier = pltpu.get_barrier_semaphore()
    peers = [(keys.at(n, 0), z) for n in (1, 2, 3)] + [(keys.at(0, n), z) for n in (1, 2, 3)] + [(keys.sibling(me), z)]
    peers += [(me, (z + n) % 8) for n in range(1, 8)]
    for peer in peers:
        pl.semaphore_signal(barrier, inc=1, device_id=peer, device_id_type=MESH)
    for k in range(GROUP_HEADS):
        @pl.when(me != z * GROUP_HEADS + k)
        def _():
            pl.semaphore_signal(barrier, inc=1, device_id=(z * GROUP_HEADS + k, z), device_id_type=MESH)

    k_cols = pl.ds(pl.multiple_of(z * HEAD_DIM, HEAD_DIM), HEAD_DIM)
    v_cols = pl.ds(pl.multiple_of(z * HEAD_DIM + KV_HEADS * HEAD_DIM, HEAD_DIM), HEAD_DIM)
    q_cols = pl.ds(pl.multiple_of(z * GROUP_HEADS * HEAD_DIM, GROUP_HEADS * HEAD_DIM), GROUP_HEADS * HEAD_DIM)
    k_local = pltpu.make_async_copy(kv_hbm.at[:, k_cols], k_buf.at[me, pl.ds(0, ROWS)], local_sem.at[0])
    v_local = pltpu.make_async_copy(kv_hbm.at[:, v_cols], v_buf.at[me], local_sem.at[1])
    q_local = pltpu.make_async_copy(q_hbm.at[:, q_cols], q_ref, local_sem.at[2])
    k_local.start()
    v_local.start()
    q_local.start()

    width = codes_ref.shape[1]
    tile = lax.broadcasted_iota(jnp.int32, (128, width), 0)
    eye = lax.broadcasted_iota(jnp.int32, (128, 128), 0) == lax.broadcasted_iota(jnp.int32, (128, 128), 1)
    named = []
    for n in range(2):
        group = jnp.broadcast_to(codes_ref[...], (128, width)) - (tile + n * 128) * NGROUP
        bits = jnp.where((group >= 0) & (group < NGROUP), lax.shift_left(1, jnp.clip(group, 0, NGROUP - 1)), 0)
        column = jnp.sum(bits, axis=1, keepdims=True)
        named.append(jnp.sum(jnp.where(eye, jnp.broadcast_to(column, (128, 128)), 0), axis=0, keepdims=True))
    parts[z] = jnp.concatenate(named + [jnp.zeros((6, 128), jnp.int32)], axis=0)

    @pl.when(z != owner)
    def _():
        pl.semaphore_wait(barrier, len(peers))

    @pl.when(z == owner)
    def _():
        pl.semaphore_wait(barrier, len(peers) + N_SEQ - 1)

    part = pltpu.make_async_remote_copy(
        src_ref=parts.at[z], dst_ref=parts.at[z], send_sem=part_send, recv_sem=part_recv.at[z],
        device_id=(me, owner), device_id_type=MESH)

    @pl.when(z != owner)
    def _():
        part.start()

    k_local.wait()
    keys.own()
    mine = me % GROUP_HEADS

    def plan_copy(k, n):
        return pltpu.make_async_remote_copy(
            src_ref=plan.at[k], dst_ref=plan.at[k], send_sem=plan_send.at[n], recv_sem=plan_recv.at[k],
            device_id=((me + n) % N_SEQ, z), device_id_type=MESH)

    @pl.when(z != owner)
    def _():
        part.wait_send()

    @pl.when(z == owner)
    def _():
        for n in range(1, 8):
            other = (z + n) % 8
            pltpu.make_async_remote_copy(
                src_ref=parts.at[other], dst_ref=parts.at[other], send_sem=part_send, recv_sem=part_recv.at[other],
                device_id=(me, other), device_id_type=MESH).wait_recv()
        total = parts[0]
        for n in range(1, 8):
            total += parts[n]
        plan[mine] = total
        plan[mine, 2:3, 0:NVERT] = verts_ref[...]
        plan[mine, 3:4, 0:NVERT] = slashes_ref[...]
        for n in range(1, N_SEQ):
            plan_copy(mine, n).start()

    keys.sends()
    v_local.wait()
    values.own()
    for k in range(GROUP_HEADS):
        @pl.when(me != z * GROUP_HEADS + k)
        def _():
            plan_copy(k, 1).wait_recv()
    slots_copy = pltpu.make_async_copy(plan, slots, local_sem.at[3])
    slots_copy.start()
    make_bias(first_tile, plan, bias_v, bias_s)
    keys.ends()
    slots_copy.wait()
    q_local.wait()
    values.near(-1, 1)
    keys.last()

    def gap(n):
        if n == 0:
            values.pass_on(0)
            values.near(2)
        elif n == 2:
            values.pass_on(-1)
            values.pass_on(1)
        elif n == 4:
            values.far(0)
            values.pass_on(2)
        elif n == 5:
            values.far(-1)
            values.far(1)
            values.far(2)
            values.last()

    def out_copy(k, n):
        other = (z + n) % 8
        return pltpu.make_async_remote_copy(
            src_ref=out_buf.at[k, pl.ds(pl.multiple_of(other * TILE, TILE), TILE)],
            dst_ref=out_ref.at[:, pl.ds(pl.multiple_of((z * GROUP_HEADS + k) * HEAD_DIM, HEAD_DIM), HEAD_DIM)],
            send_sem=out_send.at[k, n], recv_sem=out_recv.at[z, k], device_id=(me, other), device_id_type=MESH)

    @pl.loop(0, 2 * GROUP_HEADS)
    def _(step):
        @pl.when((step < 3) | (step == 6))
        def _():
            k = step - 3 * (step // 6)
            score_vertical(k, first_tile, q_ref, k_buf, slots, bias_v, score_v)

            @pl.loop(0, TILES_LOCAL // BATCH)
            def _(batch):
                tiles = [batch * BATCH + n for n in range(BATCH)]
                score_tiles(k, tiles, first_tile, q_ref, k_buf, slots, bias_s, score_v, p_v, p_s, ell)
                for n in (0, 2, 4, 5):
                    @pl.when(k * (TILES_LOCAL // BATCH) + batch == n)
                    def _():
                        gap(n)

        @pl.when(((step > 2) & (step < 6)) | (step == 7))
        def _():
            k = step - 3 - step // 7
            value_head(k, first_tile, z, v_buf, slots, p_v, p_s, ell, acc, out_buf, lambda k, n: out_copy(k, n).start())
            cols = pl.ds(pl.multiple_of((z * GROUP_HEADS + k) * HEAD_DIM, HEAD_DIM), HEAD_DIM)
            out_ref[:, cols] = out_buf[k, pl.ds(pl.multiple_of(z * TILE, TILE), TILE), :]

    keys.drain()
    values.drain()

    @pl.when(z == owner)
    def _():
        for n in range(1, N_SEQ):
            plan_copy(mine, n).wait_send()

    @pl.loop(0, GROUP_HEADS)
    def _(k):
        for n in range(1, 8):
            other = (z + n) % 8
            cols = pl.ds(pl.multiple_of((other * GROUP_HEADS + k) * HEAD_DIM, HEAD_DIM), HEAD_DIM)
            pltpu.make_async_remote_copy(
                src_ref=out_buf.at[k, pl.ds(0, TILE)], dst_ref=out_ref.at[:, cols],
                send_sem=out_send.at[k, n], recv_sem=out_recv.at[other, k], device_id=(me, other),
                device_id_type=MESH).wait_recv()
            out_copy(k, n).wait_send()


def per_device(queries, keys_values, verticals, slashes, units):
    vmem = pl.BlockSpec(memory_space=pltpu.VMEM)
    hbm = pl.BlockSpec(memory_space=pl.ANY)
    dma = pltpu.SemaphoreType.DMA
    seq = lax.axis_size("seq")
    return pl.pallas_call(
        fused_kernel,
        out_shape=jax.ShapeDtypeStruct((TILE, HEADS * HEAD_DIM), jnp.bfloat16),
        in_specs=[hbm, hbm, vmem, vmem, vmem],
        out_specs=vmem,
        scratch_shapes=[
            pltpu.VMEM((seq, ROWS, HEAD_DIM), jnp.bfloat16),
            pltpu.VMEM((seq, ROWS, HEAD_DIM), jnp.bfloat16),
            pltpu.VMEM((ROWS, GROUP_HEADS * HEAD_DIM), jnp.bfloat16),
            pltpu.VMEM((8, 8, 128), jnp.int32),
            pltpu.VMEM((GROUP_HEADS, 8, 128), jnp.int32),
            pltpu.SMEM((GROUP_HEADS, 8, 128), jnp.int32),
            pltpu.VMEM((GROUP_HEADS, TILES_LOCAL, 1, KEYS), jnp.float32),
            pltpu.VMEM((GROUP_HEADS, TILES_LOCAL, 1, KEYS), jnp.float32),
            pltpu.VMEM((ROWS, KEYS), jnp.float32),
            pltpu.VMEM((GROUP_HEADS, ROWS, KEYS), jnp.bfloat16),
            pltpu.VMEM((GROUP_HEADS, ROWS, KEYS), jnp.bfloat16),
            pltpu.VMEM((GROUP_HEADS, ROWS, HEAD_DIM), jnp.float32),
            pltpu.VMEM((ROWS, HEAD_DIM), jnp.float32),
            pltpu.VMEM((GROUP_HEADS, ROWS, HEAD_DIM), jnp.bfloat16),
            dma((4,)), dma, dma((8,)), dma((N_SEQ,)), dma((GROUP_HEADS,)),
            dma((N_SENDS,)), dma((seq, 2)), dma((N_SENDS,)), dma((seq, 2)),
            dma((GROUP_HEADS, 8)), dma((8, GROUP_HEADS)),
        ],
        compiler_params=pltpu.CompilerParams(
            vmem_limit_bytes=56 * 1024 * 1024, collective_id=0, has_side_effects=True),
        name="fused_attention",
    )(queries, keys_values, verticals, slashes, units[0])


def solution(mesh):
    in_specs = (
        P("seq", None),
        P("seq", None),
        P("seq", None),
        P("seq", None),
        P("seq", "help", None),
    )
    out_specs = P(("seq", "help"), None)
    return jax.shard_map(
        per_device, mesh=mesh, in_specs=in_specs, out_specs=out_specs, check_vma=False
    )
```
